512 devices in a mesh: section: 8 (over x, core), expert: 16 (over z), dp: 4 (over y).
Axes of the slice: x: 4, y: 4, z: 16, core: 2. Of those that a mesh axis runs over, the one named last changes fastest.
Arguments:
- frames: bfloat16 [4, 128, 48, 1280], P(None, ('expert', 'dp')), may hold values from -6 to 6
- norm_gain: float32 [8, 1280], P('section'), may hold values from 0.1 to 1.9
- router: bfloat16 [8, 1280, 16], P('section'), may hold values from -0.15625 to 0.15625
- w_in: bfloat16 [8, 16, 1280, 256], P('section', 'expert'), may hold values from -0.15625 to 0.15625
- w_out: bfloat16 [8, 16, 256, 1280], P('section', 'expert'), may hold values from -0.375 to 0.375
- routing: int32 [8, 4, 128, 48, 1], P('section', None, ('expert', 'dp')), may hold values from 0 to 15; in each aligned block of 96 rows (0 to 95, 96 to 191, ..., all dimensions but the last counted through in order) at most 7 rows name the same one
- head_gain: float32 [1280], replicated, may hold values from 0.1 to 1.9
- head_weight: bfloat16 [1280, 8000], P(None, 'expert'), may hold values from -6 to 6
- frame_lengths: int32 [4, 128], P(None, ('expert', 'dp')), may hold values from 24 to 48
- labels: int32 [4, 128, 12], P(None, ('expert', 'dp')), may hold values from 1 to 7999
- label_lengths: int32 [4, 128], P(None, ('expert', 'dp')), may hold values from 1 to 12
Outputs:
- losses: float32 [8, 64], P('section', ('expert', 'dp'))
- head_grad: bfloat16 [1280, 8000], P(None, 'expert')
The draws below stay inside these ranges and needn't reach their ends.
Inputs may be any that keep to these rules, and one draw needn't show every extreme that they name: `routing`: in each layer and micro-batch, within the frames of one device (aligned blocks of 96 frames), no expert is named by more than 7 frames.
All inputs are finite; a program needn't handle non-finite values.
Results may differ from the reference program's by a relative error of at most 0.015.
Values may be sent and summed in bfloat16 or wider, within the bound.
A program may use at most 64 MiB of HBM per device.

```python
import math
import jax
import jax.numpy as jnp
import numpy as np
from jax import lax

D = 1280
EFF = 256
VOCAB = 8000
MICRO = 4
UTT_DEV = 2
FRAMES = 48
LMAX = 12
EXPERTS = 16
TOK_DEV = 96
CAP = 7
UTTS = 128
PAIRS = 8
EXT = 25
N_SECTION = 8


def draw_head_weight(key, part):
    key = jax.random.fold_in(key, 11)
    key_base = jax.random.fold_in(key, 0)
    weight = jax.random.normal(key_base, (D, VOCAB), jnp.float32) * (3.0 / math.sqrt(D))
    return jnp.clip(weight, -6.0, 6.0).astype(jnp.bfloat16)


def draw_frame_lengths(key, part):
    key = jax.random.fold_in(key, 21)
    key_value, key_spot = jax.random.split(key)
    counts = jax.random.randint(key_value, (MICRO * UTTS,), FRAMES // 2, FRAMES + 1)
    chosen = jax.random.randint(key_spot, (), 0, MICRO * UTTS)
    counts = jnp.where(jnp.arange(MICRO * UTTS) == chosen, FRAMES, counts)
    return counts.reshape(MICRO, UTTS).astype(jnp.int32)


def draw_label_lengths(key, part):
    key = jax.random.fold_in(key, 31)
    key_value, key_spot = jax.random.split(key)
    counts = jax.random.randint(key_value, (MICRO * UTTS,), 1, LMAX + 1)
    chosen = jax.random.randint(key_spot, (), 0, MICRO * UTTS)
    counts = jnp.where(jnp.arange(MICRO * UTTS) == chosen, LMAX, counts)
    return counts.reshape(MICRO, UTTS).astype(jnp.int32)


def plant(array, key, least, high):
    longest = array.shape.index(max(array.shape))
    spots = []
    for shift in (0, 1):
        where = [jax.random.randint(jax.random.fold_in(key, axis), (), 0, length) for axis, length in enumerate(array.shape)]
        where[longest] = (where[longest] + shift) % array.shape[longest]
        spots.append(tuple(where))
    return array.at[spots[0]].set(least).at[spots[1]].set(high)


def shard_levels(rng, dims, shards, smallest, high):
    level, own = 1.0, jax.random.fold_in(rng, 6)
    for axis_at, shards_of in shards:
        steps = jnp.exp(jax.random.uniform(jax.random.fold_in(own, axis_at), (shards_of,), jnp.float32, smallest / len(shards), high / len(shards)))
        level = level * jnp.repeat(steps, dims[axis_at] // shards_of).reshape([-1 if axis == axis_at else 1 for axis in range(len(dims))])
    return level


def routed_block(key, own, number, rows, count, top, reach, skew):
    ranking = jax.random.permutation(key, count)
    packed, usual = load_shares(count, rows * top, reach, skew, True), load_shares(count, rows * top, reach, skew, False)
    places = jnp.arange(count)

    def named(sizes, turn):
        used = int((sizes > 0).sum())
        fixed = max(1, used // 4)
        moved = fixed + (places - fixed + turn * (used - fixed)) % max(1, count - fixed)
        return jnp.zeros((count,), jnp.int32).at[ranking[jnp.where(places < fixed, places, moved)]].set(jnp.asarray(sizes, jnp.int32))

    sizes = jnp.where(number % 4 == 0, named(packed, number // 4), named(usual, number - number // 4 - 1))
    mixed = jax.random.permutation(jax.random.fold_in(own, 3), count)
    donor, sink = mixed[0:count // 2 * 2:2], mixed[1:count // 2 * 2:2]
    margin = jnp.minimum(sizes[donor] - 1, reach - sizes[sink]) // 2
    margin = jnp.where((donor == ranking[0]) | (sink == ranking[0]) | (sizes[sink] == 0), 0, jnp.maximum(margin, 0))
    moved = jax.random.randint(jax.random.fold_in(own, 4), (count // 2,), 0, 1 << 20) % (margin + 1)
    sizes = sizes.at[donor].add(-moved).at[sink].add(moved)
    items = jnp.searchsorted(jnp.cumsum(sizes), jnp.arange(rows * top), side="right").astype(jnp.int32)
    listing = items.reshape(top, rows).T
    listing = listing[jax.random.permutation(jax.random.fold_in(own, 1), rows)]
    turn = jax.random.randint(jax.random.fold_in(own, 2), (rows, 1), 0, top)
    return jnp.take_along_axis(listing, (jnp.arange(top)[None, :] + turn) % top, axis=1)


def load_shares(amount, total, limit, lean, full):
    loads = [(1 << 20) // math.isqrt(standing ** lean) + 1 for standing in range(1, amount + 1)]
    largest = limit if full else min(limit, max(-(-total // amount), total * loads[0] // sum(loads)))
    least = 1 if total - largest >= amount - 1 else 0
    given, rest = [largest] + [least] * (amount - 1), total - largest - least * (amount - 1)
    while rest > 0:
        free = [i for i in range(1, amount) if given[i] < largest] or [i for i in range(1, amount) if given[i] < limit]
        whole, remaining = sum([loads[i] for i in free]), rest
        for i in free:
            addition = min(limit - given[i], max(1, remaining * loads[i] // whole), rest)
            given[i] = given[i] + addition
            rest = rest - addition
    return np.array(given)


def normal_values(key, extent, scale, bound, cuts=(), kind=jnp.bfloat16):
    loudness = shard_levels(key, extent, cuts, -0.22, 0.18) if cuts else 1.0
    values = jax.random.normal(key, extent, jnp.float32) * scale * loudness
    return jnp.minimum(jnp.maximum(values, -bound), bound).astype(kind)


def setup_inputs(seed: int = 0) -> dict:
    key_of = jax.random.split(jax.random.key(seed), 12)
    frames = normal_values(key_of[0], (MICRO, UTTS, FRAMES, D), 1.0, 6.0, ((1, 64),))
    norm_gain = jnp.clip(1.0 + 0.18 * jax.random.normal(key_of[1], (N_SECTION, D), jnp.float32), 0.1, 1.9)
    router = normal_values(key_of[2], (N_SECTION, D, EXPERTS), D ** -0.5, 0.15625, ((0, 8),))
    w_in = normal_values(key_of[3], (N_SECTION, EXPERTS, D, EFF), D ** -0.5, 0.15625, ((0, 8), (1, 16)))
    w_out = normal_values(key_of[4], (N_SECTION, EXPERTS, EFF, D), EFF ** -0.5, 0.375, ((0, 8), (1, 16)))
    routing_keys = jax.random.split(jax.random.fold_in(key_of[5], 1), N_SECTION * MICRO * UTTS * FRAMES // TOK_DEV)
    routing_turns = jax.random.permutation(jax.random.fold_in(key_of[5], 3), N_SECTION * MICRO * UTTS * FRAMES // TOK_DEV)
    routing = jax.vmap(lambda own, number: routed_block(jax.random.fold_in(key_of[5], 2), own, number, TOK_DEV, EXPERTS, 1, CAP, 2))(routing_keys, routing_turns).reshape((N_SECTION, MICRO, UTTS, FRAMES, 1))
    head_gain = jnp.clip(1.0 + 0.18 * jax.random.normal(key_of[6], (D,), jnp.float32), 0.1, 1.9)
    head_weight = draw_head_weight(jax.random.fold_in(key_of[11], 71), 0)
    frame_lengths = draw_frame_lengths(jax.random.fold_in(key_of[11], 71), 0)
    labels = plant(jax.random.randint(key_of[9], (MICRO, UTTS, LMAX), 1, VOCAB), jax.random.fold_in(key_of[9], 1), 1, VOCAB - 1).astype(jnp.int32)
    label_lengths = draw_label_lengths(jax.random.fold_in(key_of[11], 71), 0)
    return {"frames": frames, "norm_gain": norm_gain, "router": router, "w_in": w_in, "w_out": w_out, "routing": routing, "head_gain": head_gain, "head_weight": head_weight, "frame_lengths": frame_lengths, "labels": labels, "label_lengths": label_lengths}


EPSILON = 1e-06
LOG_ZERO = -1e+30

def rms_scale(values, scaling):
    values = values.astype(jnp.float32)
    return values * lax.rsqrt(lax.optimization_barrier(jnp.mean(values * values, axis=-1, keepdims=True)) + EPSILON) * scaling

def slot_index(expert_ids, expert_count, capacity):
    one_hot = (expert_ids[:, None] == jnp.arange(expert_count, dtype=jnp.int32)[None, :]).astype(jnp.int32)
    slot_rank = lax.optimization_barrier(jnp.sum((jnp.cumsum(one_hot, axis=0) - 1) * one_hot, axis=1))
    return ((expert_ids * capacity + slot_rank).astype(jnp.int32), one_hot)

def extend_labels(label_rows):
    blanks = jnp.zeros_like(label_rows)
    paired = jnp.stack([blanks, label_rows], axis=-1).reshape(label_rows.shape[:-1] + (2 * label_rows.shape[-1],))
    return jnp.concatenate([paired, jnp.zeros(label_rows.shape[:-1] + (1,), jnp.int32)], axis=-1)

def ctc_single(emission, ext_labels, frame_count, label_count):
    state_count = ext_labels.shape[0]
    position = jnp.arange(state_count, dtype=jnp.int32)
    earlier = jnp.concatenate([jnp.full((2,), -1, jnp.int32), ext_labels[:-2]])
    skippable = (ext_labels != 0) & (ext_labels != earlier) & (position >= 2)
    lowest = jnp.full((state_count,), LOG_ZERO, emission.dtype)
    initial = jnp.where(position < 2, emission[0], lowest)

    def advance(forward_log, inputs):
        emit_row, time_step = inputs
        one_back = jnp.concatenate([lowest[:1], forward_log[:-1]])
        two_back = jnp.where(skippable, jnp.concatenate([lowest[:2], forward_log[:-2]]), lowest)
        moved = jnp.logaddexp(jnp.logaddexp(forward_log, one_back), two_back) + emit_row
        return (jnp.where(time_step < frame_count, moved, forward_log), None)
    time_steps = jnp.arange(1, emission.shape[0], dtype=jnp.int32)
    final_log, _ = lax.scan(advance, initial, (emission[1:], time_steps))
    last_state = 2 * label_count
    end_state = jnp.sum(jnp.where(position == last_state, final_log, 0.0))
    near_state = jnp.sum(jnp.where(position == last_state - 1, final_log, 0.0))
    return -jnp.logaddexp(end_state, near_state)

def ctc_terms(emission, ext_labels, frame_counts, label_counts):

    def summed_loss(values):
        losses = jax.vmap(ctc_single)(values, ext_labels, frame_counts, label_counts)
        return (jnp.sum(losses), losses)
    summed, pullback, losses = jax.vjp(summed_loss, emission, has_aux=True)
    occupancy = pullback(jnp.ones_like(summed))[0]
    return (losses, occupancy)

def moe_section(current_rows, layer_routes, scaling, router_w, weight_in, weight_out, capacity):
    expert_count = router_w.shape[1]
    block_count, tokens, width = current_rows.shape
    normed = rms_scale(current_rows, scaling).astype(jnp.bfloat16)
    logits = jnp.einsum('btd,de->bte', normed.astype(jnp.float32), router_w.astype(jnp.float32))
    target_slot, one_hot = jax.vmap(lambda routes: slot_index(routes, expert_count, capacity))(layer_routes)
    gate_value = jax.nn.sigmoid(lax.optimization_barrier(jnp.sum(jnp.where(one_hot > 0, logits, 0.0), axis=-1)))

    def place_rows(row_values, slots):
        return jnp.zeros((expert_count * capacity, width), jnp.bfloat16).at[slots].set(row_values)
    buffers = jax.vmap(place_rows)(normed, target_slot).reshape(block_count, expert_count, capacity, width)
    hidden = jnp.einsum('becd,edh->bech', buffers.astype(jnp.float32), weight_in.astype(jnp.float32))
    active = (hidden * jax.nn.sigmoid(hidden)).astype(jnp.bfloat16)
    outputs = jnp.einsum('bech,ehd->becd', active.astype(jnp.float32), weight_out.astype(jnp.float32)).astype(jnp.bfloat16)
    outputs = outputs.reshape(block_count, expert_count * capacity, width)
    picked = jax.vmap(lambda row_values, slots: row_values[slots])(outputs, target_slot)
    return (current_rows.astype(jnp.float32) + gate_value[..., None] * picked.astype(jnp.float32)).astype(jnp.bfloat16)

def reference(frames, norm_gain, router, w_in, w_out, routing, head_gain, head_weight, frame_lengths, labels, label_lengths):
    group_count = UTTS // UTT_DEV
    tokens = UTT_DEV * FRAMES
    hidden_state = frames.reshape(MICRO * group_count, tokens, D)
    for layer_index in range(N_SECTION):
        layer_routes = routing[layer_index, :, :, :, 0].reshape(MICRO * group_count, tokens)
        hidden_state = moe_section(hidden_state, layer_routes, norm_gain[layer_index], router[layer_index], w_in[layer_index], w_out[layer_index], CAP)
    final_rows = hidden_state.reshape(MICRO * UTTS, FRAMES, D)
    ext_all = extend_labels(labels.reshape(MICRO * UTTS, LMAX))
    frame_all = frame_lengths.reshape(MICRO * UTTS)
    label_all = label_lengths.reshape(MICRO * UTTS)
    block_size = 8
    block_total = MICRO * UTTS // block_size

    def head_block(grad_sum, inputs):
        hidden_rows, ext_rows, frame_rows, label_rows = inputs
        normed = rms_scale(hidden_rows, head_gain).astype(jnp.bfloat16)
        flat_rows = normed.reshape(block_size * FRAMES, D)
        logits = jnp.dot(flat_rows, head_weight, preferred_element_type=jnp.float32)
        highest = lax.optimization_barrier(jnp.max(logits, axis=1, keepdims=True))
        log_total = highest + jnp.log(lax.optimization_barrier(jnp.sum(jnp.exp(logits - highest), axis=1, keepdims=True)))
        logprob = (logits - log_total).reshape(block_size, FRAMES, VOCAB)
        selector = (ext_rows[:, :, None] == jnp.arange(VOCAB, dtype=jnp.int32)[None, None, :]).astype(jnp.float32)
        emission = jnp.einsum('btv,bsv->bts', logprob, selector, precision=lax.Precision.HIGHEST)
        losses, occupancy = ctc_terms(emission, ext_rows, frame_rows, label_rows)
        scattered = jnp.einsum('bts,bsv->btv', occupancy, selector, precision=lax.Precision.HIGHEST)
        grad_logits = (scattered - jnp.exp(logprob) * lax.optimization_barrier(jnp.sum(occupancy, axis=2, keepdims=True))).astype(jnp.bfloat16)
        grad_sum = grad_sum + lax.dot_general(flat_rows, grad_logits.reshape(block_size * FRAMES, VOCAB), (((0,), (0,)), ((), ())), preferred_element_type=jnp.float32)
        return (grad_sum, losses)
    grad_total, block_losses = lax.scan(head_block, jnp.zeros((D, VOCAB), jnp.float32), (final_rows.reshape(block_total, block_size, FRAMES, D), ext_all.reshape(block_total, block_size, EXT), frame_all.reshape(block_total, block_size), label_all.reshape(block_total, block_size)))
    loss_table = block_losses.reshape(MICRO, group_count, UTT_DEV).transpose(0, 2, 1).reshape(PAIRS, group_count)
    return (loss_table, grad_total.astype(jnp.bfloat16))
```

```python
import functools

import jax
import jax.numpy as jnp
from jax import lax
from jax.experimental import pallas as pl
from jax.experimental.pallas import tpu as pltpu
from jax.sharding import PartitionSpec as P

EPSILON = 1e-06
LOG_ZERO = -1e30
MESH = pl.DeviceIdType.MESH
F32, BF16 = jnp.float32, jnp.bfloat16
D, HALF, EFF, LAYERS, RING, TOK, FRAMES = 1280, 640, 256, 8, 16, 96, 48
PIECES = 8
CHUNKS = LAYERS * PIECES
IN_ROWS, OUT_ROWS = D // PIECES, EFF // PIECES
SHARD, WIDE = 500, 512
HIGHEST = lax.Precision.HIGHEST
VMEM = pltpu.VMEM
DMA = pltpu.SemaphoreType.DMA
VMEM_LIMIT = 56 * 1024 * 1024


def coords():
    s, z, y = lax.axis_index("section"), lax.axis_index("expert"), lax.axis_index("dp")
    return s, s // 2, lax.rem(s, 2), z, y


def loop(low, high, body):
    def step(i, carry):
        body(i)
        return carry

    lax.fori_loop(low, high, step, 0)


def remote(src, dst, send, recv, device):
    return pltpu.make_async_remote_copy(
        src_ref=src, dst_ref=dst, send_sem=send, recv_sem=recv, device_id=device, device_id_type=MESH
    )


def dot(a, b, dims=((1,), (0,)), precision=None):
    return lax.dot_general(a, b, (dims, ((), ())), precision=precision, preferred_element_type=F32)


def rms(x, gain):
    return (x * lax.rsqrt(jnp.mean(x * x, axis=-1, keepdims=True) + EPSILON) * gain).astype(BF16)


def moe_kernel(
    x0, w_in, w_out, router, aux, head_gain, hn_out,
    win, wout, routers, auxes, state, give, take, answer, back, stage_in, stage_out, passed, landed,
    got_in, got_out, on_in, on_out, copy_in, copy_out, have_in, have_out,
    lay_send, stage_send, stage_got, small_send, small_got, give_send, take_got, answer_send, back_got, hn_send, hn_got,
):
    s, x, c, z, y = coords()
    me = 4 * x + y
    home_x, home_y = z // 4, lax.rem(z, 4)
    above, below = lax.rem(z + 1, RING), lax.rem(z + RING - 1, RING)
    barrier = pltpu.get_barrier_semaphore()

    def greet(i):
        p = lax.rem(4 * s + y + i, 32)
        pl.semaphore_signal(barrier, inc=1, device_id=(p // 4, z, lax.rem(p, 4)), device_id_type=MESH)

    loop(1, 32, greet)
    pl.semaphore_signal(barrier, inc=1, device_id=(s, above, y), device_id_type=MESH)
    pl.semaphore_signal(barrier, inc=1, device_id=(s, below, y), device_id_type=MESH)
    pl.semaphore_wait(barrier, 33)

    def in_rows(j):
        return pl.ds(pl.multiple_of(j * IN_ROWS, 32), IN_ROWS)

    def out_rows(j):
        return pl.ds(pl.multiple_of(j * OUT_ROWS, 32), OUT_ROWS)

    def share(layer, i, src_in, src_out):
        j = y + 4 * i
        k = layer * PIECES + j
        target = (2 * home_x + 1, z, home_y)
        return (
            remote(src_in, win.at[layer, in_rows(j)], lay_send.at[2 * c, i], got_in.at[k], target),
            remote(src_out, wout.at[layer, out_rows(j)], lay_send.at[2 * c + 1, i], got_out.at[k], target),
        )

    def staged(i):
        j = y + 4 * i
        target = (s + 1, z, y)
        return (
            remote(w_in.at[in_rows(j)], stage_in.at[i], stage_send.at[0, i], stage_got.at[0, i], target),
            remote(w_out.at[out_rows(j)], stage_out.at[i], stage_send.at[1, i], stage_got.at[1, i], target),
        )

    def small(to_x):
        target = (2 * to_x, z, y)
        return (
            remote(aux, auxes.at[s], small_send.at[0, to_x], small_got.at[0, s], target),
            remote(router, routers.at[s], small_send.at[1, to_x], small_got.at[1, s], target),
        )

    def each(copies, act):
        for copy in copies:
            act(copy)

    start, sent, got = (lambda d: d.start()), (lambda d: d.wait_send()), (lambda d: d.wait_recv())

    @pl.when((c == 0) & (x == 0))
    def _():
        for i in range(2):
            each(share(0, i, w_in.at[in_rows(y + 4 * i)], w_out.at[out_rows(y + 4 * i)]), start)

    @pl.when((c == 0) & (x > 0))
    def _():
        for i in range(2):
            each(staged(i), start)

    for gap in range(1, 4):
        each(small(lax.rem(x + gap, 4)), start)

    own_small = (
        pltpu.make_async_copy(aux, auxes.at[s], small_got.at[0, s]),
        pltpu.make_async_copy(router, routers.at[s], small_got.at[1, s]),
    )

    @pl.when(c == 1)
    def _():
        each(small(x), start)

    @pl.when(c == 0)
    def _():
        each(own_small, start)

    @pl.when(c == 1)
    def _():
        at_home = (x == home_x) & (y == home_y)
        up, down = lax.rem(z + RING - me, RING), lax.rem(me + RING - z, RING)

        def distribute(layer, slot, pick):
            for i in range(2):
                j = y + 4 * i
                src_in, src_out = pick(i)

                @pl.when(at_home)
                def _():
                    k = layer * PIECES + j
                    pltpu.make_async_copy(src_in, win.at[layer, in_rows(j)], got_in.at[k]).start()
                    pltpu.make_async_copy(src_out, wout.at[layer, out_rows(j)], got_out.at[k]).start()

                @pl.when(jnp.logical_not(at_home))
                def _():
                    each(carried(layer, slot, i, src_in, src_out), start)

        def carried(layer, slot, i, src_in, src_out):
            j = y + 4 * i
            k = layer * PIECES + j
            target = (2 * home_x + 1, z, home_y)
            return (
                remote(src_in, win.at[layer, in_rows(j)], lay_send.at[2 * slot, i], got_in.at[k], target),
                remote(src_out, wout.at[layer, out_rows(j)], lay_send.at[2 * slot + 1, i], got_out.at[k], target),
            )

        def from_stage(i):
            return stage_in.at[i], stage_out.at[i]

        def from_own(i):
            return w_in.at[in_rows(y + 4 * i)], w_out.at[out_rows(y + 4 * i)]

        def rise(k):
            layer, j = k // PIECES, lax.rem(k, PIECES)
            ref = win.at[layer, in_rows(j)]
            return remote(ref, ref, on_in.at[k], got_in.at[k], (s, above, y))

        def sink(k):
            layer, j = k // PIECES, lax.rem(k, PIECES)
            ref = wout.at[layer, out_rows(j)]
            return remote(ref, ref, on_out.at[k], got_out.at[k], (s, below, y))

        def hand_in(layer):
            return remote(win.at[layer], win.at[layer], copy_in.at[layer], have_in.at[layer], (s - 1, z, y))

        def hand_out(layer):
            return remote(wout.at[layer], wout.at[layer], copy_out.at[layer], have_out.at[layer], (s - 1, z, y))

        def tick(t):
            @pl.when((x > 0) & (t == 16 * x - 8))
            def _():
                for i in range(2):
                    each(staged(i), got)
                distribute(2 * x, 0, from_stage)

            @pl.when(t == 16 * x)
            def _():
                distribute(2 * x + 1, 1, from_own)

            ku, kd = t - up, t - down

            @pl.when((ku >= 0) & (ku < CHUNKS))
            def _():
                rise(ku).wait_recv()

                @pl.when(up < RING - 1)
                def _():
                    rise(ku).start()

                @pl.when(lax.rem(ku, PIECES) == PIECES - 1)
                def _():
                    hand_in(ku // PIECES).start()

            @pl.when((kd >= 0) & (kd < CHUNKS))
            def _():
                sink(kd).wait_recv()

                @pl.when(down < RING - 1)
                def _():
                    sink(kd).start()

                @pl.when(lax.rem(kd, PIECES) == PIECES - 1)
                def _():
                    hand_out(kd // PIECES).start()

        loop(0, CHUNKS + RING - 1, tick)

        @pl.when(jnp.logical_not(at_home))
        def _():
            for i in range(2):
                @pl.when(x > 0)
                def _():
                    each(carried(2 * x, 0, i, *from_stage(i)), sent)

                each(carried(2 * x + 1, 1, i, *from_own(i)), sent)

        @pl.when(up < RING - 1)
        def _():
            loop(0, CHUNKS, lambda k: rise(k).wait_send())

        @pl.when(down < RING - 1)
        def _():
            loop(0, CHUNKS, lambda k: sink(k).wait_send())

        loop(0, LAYERS, lambda layer: hand_in(layer).wait_send())
        loop(0, LAYERS, lambda layer: hand_out(layer).wait_send())
        each(small(x), sent)

    @pl.when(c == 0)
    def _():
        state[...] = x0[...]

        def smalls(layer):
            pltpu.make_async_copy(aux, auxes.at[layer], small_got.at[0, layer]).wait()
            pltpu.make_async_copy(router, routers.at[layer], small_got.at[1, layer]).wait()

        loop(0, LAYERS, smalls)

        def chip(p):
            return (2 * (p // 4), z, lax.rem(p, 4))

        def out_to(p):
            return remote(give.at[p], take.at[me], give_send.at[p], take_got.at[me], chip(p))

        def in_from(p):
            return remote(give.at[p], take.at[p], give_send.at[p], take_got.at[p], chip(p))

        def back_to(p):
            return remote(answer.at[p], back.at[me], answer_send.at[p], back_got.at[me], chip(p))

        def back_from(p):
            return remote(answer.at[p], back.at[p], answer_send.at[p], back_got.at[p], chip(p))

        def others(act):
            loop(1, RING, lambda i: act(lax.rem(me + i, RING)))

        def layer_step(layer):
            xf = state[...].astype(F32)
            normed = rms(xf, auxes[layer, 0:1, :])
            which = lax.broadcasted_iota(jnp.int32, (8, 128), 0) == 1 + x
            spots = jnp.sum(jnp.where(which, auxes[layer, :, 0:128], 0.0), axis=0, keepdims=True)
            pick = (lax.broadcasted_iota(jnp.int32, (128, 128), 0).astype(F32) == spots)[:, :TOK]
            pick = pick.astype(F32).astype(BF16)
            left = dot(pick, normed[:, :HALF]).reshape(RING, 8, HALF)
            right = dot(pick, normed[:, HALF:]).reshape(RING, 8, HALF)
            give[...] = jnp.concatenate([left, right], axis=1).astype(BF16)
            others(lambda p: out_to(p).start())
            take[me] = give[me]

            columns = jnp.transpose(jnp.broadcast_to(spots, (128, 128)))[:TOK, :].astype(jnp.int32)
            lane = lax.broadcasted_iota(jnp.int32, (TOK, 128), 1)
            logits = dot(normed, routers[layer], ((1,), (1,)))
            mine = (lane[:, :RING] == (columns[:, :RING] >> 3)).astype(F32)
            gate = jax.nn.sigmoid(jnp.sum(mine * logits, axis=1, keepdims=True))
            place = columns + ((columns >> 3) << 3)
            spread = [(lane + 128 * h == place + 8 * b).astype(F32).astype(BF16) for b in range(2) for h in range(2)]
            put_left = jnp.concatenate(spread[:2], axis=1)
            put_right = jnp.concatenate(spread[2:], axis=1)

            pltpu.make_async_copy(win.at[layer], win.at[layer], have_in.at[layer]).wait()
            others(lambda p: in_from(p).wait_recv())
            rows = take[...].reshape(RING * 16, HALF)
            first = dot(rows, win[layer, 0:HALF, :]).reshape(RING, 16, EFF)
            second = dot(rows, win[layer, HALF:D, :]).reshape(RING, 16, EFF)
            hidden = (first[:, 0:8] + second[:, 8:16]).reshape(128, EFF)
            active = (hidden * jax.nn.sigmoid(hidden)).astype(BF16)
            pltpu.make_async_copy(wout.at[layer], wout.at[layer], have_out.at[layer]).wait()
            result = dot(active, wout[layer]).reshape(RING, 8, D)
            answer[...] = jnp.concatenate([result[:, :, :HALF], result[:, :, HALF:]], axis=1).astype(BF16)
            others(lambda p: back_to(p).start())
            back[me] = answer[me]
            others(lambda p: out_to(p).wait_send())
            others(lambda p: back_from(p).wait_recv())
            returned = back[...].reshape(RING * 16, HALF)
            mixed = jnp.concatenate([dot(put_left, returned), dot(put_right, returned)], axis=1)
            state[...] = (xf + gate * mixed).astype(BF16)
            others(lambda p: back_to(p).wait_send())

        loop(0, LAYERS, layer_step)
        hn = rms(state[...].astype(F32), head_gain[...])
        for h in range(2):
            hn_out[h] = hn[:FRAMES, HALF * h : HALF * (h + 1)]
            passed[h] = hn[FRAMES:, HALF * h : HALF * (h + 1)]
        remote(passed, landed, hn_send, hn_got, (s + 1, z, y)).start()

        @pl.when(x == 0)
        def _():
            for i in range(2):
                each(share(0, i, w_in.at[in_rows(y + 4 * i)], w_out.at[out_rows(y + 4 * i)]), sent)

        @pl.when(x > 0)
        def _():
            for i in range(2):
                each(staged(i), sent)

        remote(passed, landed, hn_send, hn_got, (s + 1, z, y)).wait_send()

    @pl.when(c == 1)
    def _():
        remote(passed, landed, hn_send, hn_got, (s, z, y)).wait_recv()
        hn_out[...] = landed[...]

    for gap in range(1, 4):
        each(small(lax.rem(x + gap, 4)), sent)


def run_moe(x0, w_in, w_out, router, aux, head_gain):
    anywhere, local = pl.BlockSpec(memory_space=pl.ANY), pl.BlockSpec(memory_space=VMEM)
    return pl.pallas_call(
        moe_kernel,
        out_shape=jax.ShapeDtypeStruct((2, FRAMES, HALF), BF16),
        in_specs=[local, anywhere, anywhere, local, local, local],
        out_specs=local,
        scratch_shapes=[
            VMEM((LAYERS, D, EFF), BF16),
            VMEM((LAYERS, EFF, D), BF16),
            VMEM((LAYERS, 16, D), BF16),
            VMEM((LAYERS, 8, D), F32),
            VMEM((TOK, D), BF16),
            VMEM((RING, 16, HALF), BF16),
            VMEM((RING, 16, HALF), BF16),
            VMEM((RING, 16, HALF), BF16),
            VMEM((RING, 16, HALF), BF16),
            VMEM((2, IN_ROWS, EFF), BF16),
            VMEM((2, OUT_ROWS, D), BF16),
            VMEM((2, FRAMES, HALF), BF16),
            VMEM((2, FRAMES, HALF), BF16),
            DMA((CHUNKS,)), DMA((CHUNKS,)), DMA((CHUNKS,)), DMA((CHUNKS,)),
            DMA((LAYERS,)), DMA((LAYERS,)), DMA((LAYERS,)), DMA((LAYERS,)),
            DMA((4, 2)), DMA((2, 2)), DMA((2, 2)), DMA((2, 4)), DMA((2, LAYERS)),
            DMA((RING,)), DMA((RING,)), DMA((RING,)), DMA((RING,)),
            DMA, DMA,
        ],
        compiler_params=pltpu.CompilerParams(
            collective_id=0, has_side_effects=True, vmem_limit_bytes=VMEM_LIMIT
        ),
    )(x0, w_in, w_out, router, aux, head_gain)


def flip(block):
    rows = block.shape[0]
    if rows < 128:
        block = jnp.concatenate([block, jnp.zeros((128 - rows, 128), F32)], axis=0)
    return jnp.transpose(block)


def pack(columns):
    turned = flip(columns)
    return turned[0:8] + pltpu.roll(turned[8:16], 64, 1)


def lanes(rows):
    return lax.broadcasted_iota(jnp.int32, (rows, 128), 1)


def triple(a, b, c):
    top = jnp.maximum(jnp.maximum(a, b), c)
    return top + jnp.log(jnp.exp(a - top) + jnp.exp(b - top) + jnp.exp(c - top))


def head_kernel(
    hn, weight, names, meta, loss_out, grad_out,
    rows_all, names_all, logits, stats, stats_all, emit, ahead, behind, notes, notes_all, grads, partial,
    half_out, half_in, pieces, pieces_all, total, totals,
    up_send, up_got, down_send, down_got, name_send, name_got, stat_send, stat_got, note_send, note_got,
    half_send, half_got, piece_send, piece_got, total_send, total_got, last_send, last_got,
):
    s, x, c, z, y = coords()
    me = 4 * x + y
    pair = (s + 1 - 2 * c, z, y)
    above, below = lax.rem(z + 1, RING), lax.rem(z + RING - 1, RING)
    barrier = pltpu.get_barrier_semaphore()

    def chip(p):
        return (2 * (p // 4) + c, z, lax.rem(p, 4))

    def greet(i):
        pl.semaphore_signal(barrier, inc=1, device_id=(s, lax.rem(z + i, RING), y), device_id_type=MESH)
        pl.semaphore_signal(barrier, inc=1, device_id=chip(lax.rem(me + i, RING)), device_id_type=MESH)

    loop(1, RING, greet)
    pl.semaphore_signal(barrier, inc=1, device_id=pair, device_id_type=MESH)
    pl.semaphore_wait(barrier, 31)

    def along(act):
        loop(1, RING, lambda i: act(lax.rem(z + i, RING)))

    def across(act):
        loop(1, RING, lambda i: act(lax.rem(me + i, RING)))

    def rise(i, h):
        block = rows_all.at[lax.rem(z + RING - i, RING), h]
        return remote(block, block, up_send.at[i, h], up_got.at[i, h], (s, above, y))

    def sink(i, h):
        block = rows_all.at[lax.rem(z + i, RING), h]
        return remote(block, block, down_send.at[i, h], down_got.at[i, h], (s, below, y))

    def risen(i, h):
        block = rows_all.at[lax.rem(z + RING - i, RING), h]
        return remote(block, block, up_send.at[i - 1, h], up_got.at[i - 1, h], (s, above, y))

    def sunk(i, h):
        block = rows_all.at[lax.rem(z + i, RING), h]
        return remote(block, block, down_send.at[i - 1, h], down_got.at[i - 1, h], (s, below, y))

    rows_all[z] = hn[...]
    names_all[z] = names[...]
    for h in range(2):
        rise(0, h).start()
        sink(0, h).start()

    def name_to(p):
        return remote(names, names_all.at[z], name_send.at[p], name_got.at[z], (s, p, y))

    def name_from(p):
        return remote(names, names_all.at[p], name_send.at[p], name_got.at[p], (s, p, y))

    along(lambda p: name_to(p).start())

    def ring_step(i):
        for h in range(2):
            risen(i, h).wait_recv()

            @pl.when(i < 8)
            def _():
                rise(i, h).start()

            @pl.when(i < 8)
            def _():
                sunk(i, h).wait_recv()

            @pl.when(i < 7)
            def _():
                sink(i, h).start()

    loop(1, 9, ring_step)
    along(lambda p: name_from(p).wait_recv())

    def product(b):
        columns = pl.ds(pl.multiple_of(b * 256, 256), 256)
        logits[:, columns] = dot(rows_all[:, 0].reshape(RING * FRAMES, HALF), weight[0:HALF, columns]) + dot(
            rows_all[:, 1].reshape(RING * FRAMES, HALF), weight[HALF:D, columns]
        )

    loop(0, WIDE // 256, product)

    columns = lax.broadcasted_iota(jnp.int32, (128, WIDE), 1)
    valid = columns[:FRAMES] < SHARD
    owned = jnp.where(columns < SHARD, columns + SHARD * z, -1).astype(F32)

    def selector(k):
        wanted = flip(jnp.broadcast_to(names_all[k, 0:1, :], (128, 128)))
        return (jnp.concatenate([wanted] * 4, axis=1) == owned).astype(F32)

    def frames_of(k):
        return pl.ds(pl.multiple_of(k * FRAMES, FRAMES), FRAMES)

    lane = lanes(FRAMES)

    def gather_stats(k):
        block = logits[frames_of(k), :]
        peak = jnp.max(jnp.where(valid, block, -jnp.inf), axis=1, keepdims=True)
        weightsum = jnp.sum(jnp.where(valid, jnp.exp(block - peak), 0.0), axis=1, keepdims=True)
        found = dot(block, selector(k), ((1,), (1,)), HIGHEST)
        stats[k] = pack(jnp.where(lane == 13, peak, jnp.where(lane == 14, weightsum, found)))

    loop(0, RING, gather_stats)
    stats_all[z] = stats[z]

    def stat_to(p):
        return remote(stats.at[p], stats_all.at[z], stat_send.at[p], stat_got.at[z], (s, p, y))

    def stat_from(p):
        return remote(stats.at[p], stats_all.at[p], stat_send.at[p], stat_got.at[p], (s, p, y))

    along(lambda p: stat_to(p).start())
    along(lambda p: stat_from(p).wait_recv())

    low = [stats_all[k] for k in range(RING)]
    high = [pltpu.roll(v, 64, 1) for v in low]
    peaks = functools.reduce(jnp.maximum, high)
    sums = sum(v * pltpu.roll(jnp.exp(v - peaks), 1, 0) for v in high)
    live = lanes(1) < FRAMES
    log_total = jnp.where(live, peaks[5:6] + jnp.log(jnp.where(live, sums[6:7], 1.0)), 0.0)
    both = jnp.concatenate([sum(low), sum(high)], axis=0)
    slot = lax.broadcasted_iota(jnp.int32, (16, 128), 0)
    both = jnp.where(lanes(16) < FRAMES, both - log_total, 0.0)
    both = jnp.where(slot < 13, both, jnp.where(slot == 14, log_total, 0.0))
    by_label = flip(both)
    row, col = lax.broadcasted_iota(jnp.int32, (128, 128), 0), lanes(128)
    odd = (col & 1) == 1
    expand = (col < 25) & (jnp.where(odd, col >> 1, 12) == row)
    expand = expand.astype(F32)
    emit[...] = dot(by_label[:FRAMES], expand, precision=HIGHEST)
    total_col = by_label[:FRAMES]
    one = lanes(1)
    span, last = meta[0:1, :], meta[1:2, :]
    jump, jump_back = meta[2:3, :] > 0, meta[3:4, :] > 0
    spot = one.astype(F32)
    ends = (spot == last) | (spot == last - 1.0)
    closing = jnp.where(ends, 0.0, LOG_ZERO)
    opening = jnp.where(one < 2, emit[0:1, :], LOG_ZERO)
    ahead[0:1, :] = opening
    behind[FRAMES - 1 : FRAMES, :] = closing

    def ctc_step(i, carry):
        a, b = carry
        once = jnp.where(one < 1, LOG_ZERO, pltpu.roll(a, 1, 1))
        twice = jnp.where(jump, pltpu.roll(a, 2, 1), LOG_ZERO)
        moved = triple(a, once, twice) + emit[pl.ds(i, 1), :]
        a = jnp.where(i.astype(F32) < span, moved, a)
        ahead[pl.ds(i, 1), :] = a
        t = FRAMES - 1 - i
        g = b + emit[pl.ds(t + 1, 1), :]
        once = jnp.where(one > 126, LOG_ZERO, pltpu.roll(g, 127, 1))
        twice = jnp.where(jump_back, pltpu.roll(g, 126, 1), LOG_ZERO)
        b = jnp.where(t.astype(F32) < span - 1.0, triple(g, once, twice), closing)
        behind[pl.ds(t, 1), :] = b
        return a, b

    final, _ = lax.fori_loop(1, FRAMES, ctc_step, (opening, closing))
    tail = jnp.where(ends, final, LOG_ZERO)
    top = jnp.max(tail, axis=1, keepdims=True)
    likely = top + jnp.log(jnp.sum(jnp.where(ends, jnp.exp(final - top), 0.0), axis=1, keepdims=True))
    loss_out[...] = jnp.broadcast_to(-likely, (8, 128))
    when = lax.broadcasted_iota(jnp.int32, (FRAMES, 128), 0).astype(F32)
    occupied = jnp.where(
        (when < span) & (lane < 25), -jnp.exp(ahead[...] + behind[...] - likely), 0.0
    )
    merged = dot(occupied, expand, ((1,), (1,)), HIGHEST)
    mass = jnp.sum(occupied, axis=1, keepdims=True)
    notes[...] = pack(
        jnp.where(lane == 13, mass, jnp.where(lane == 14, total_col, jnp.where(lane < 13, merged, 0.0)))
    )
    notes_all[z] = notes[...]

    def note_to(p):
        return remote(notes, notes_all.at[z], note_send.at[p], note_got.at[z], (s, p, y))

    def note_from(p):
        return remote(notes, notes_all.at[p], note_send.at[p], note_got.at[p], (s, p, y))

    along(lambda p: note_to(p).start())
    along(lambda p: note_from(p).wait_recv())

    def spread(k):
        packed = notes_all[k]
        known = flip(jnp.concatenate([packed, pltpu.roll(packed, 64, 1)], axis=0))[:FRAMES]
        scattered = dot(known, selector(k), precision=HIGHEST)
        block = logits[frames_of(k), :]
        value = scattered - jnp.exp(block - known[:, 14:15]) * known[:, 13:14]
        grads[frames_of(k), :] = jnp.where(valid, value, 0.0).astype(BF16)

    loop(0, RING, spread)
    for h in range(2):
        partial[:, HALF * h : HALF * (h + 1)] = dot(
            grads[...], rows_all[:, h].reshape(RING * FRAMES, HALF), ((0,), (0,))
        )

    def mine(core):
        return pl.ds(pl.multiple_of(256 * core, 256), 256)

    half_out[...] = partial[mine(1 - c), :].astype(BF16)
    swap = remote(half_out, half_in, half_send, half_got, pair)
    swap.start()
    swap.wait_recv()
    pieces[...] = (partial[mine(c), :] + half_in[...].astype(F32)).astype(BF16).reshape(RING, 16, D)

    def piece_to(p):
        return remote(pieces.at[p], pieces_all.at[me], piece_send.at[p], piece_got.at[me], chip(p))

    def piece_from(p):
        return remote(pieces.at[p], pieces_all.at[p], piece_send.at[p], piece_got.at[p], chip(p))

    across(lambda p: piece_to(p).start())
    pieces_all[me] = pieces[me]
    across(lambda p: piece_from(p).wait_recv())
    total[...] = sum(pieces_all[k].astype(F32) for k in range(RING)).astype(BF16)

    def total_to(p):
        return remote(total, totals.at[c, me], total_send.at[p], total_got.at[me], chip(p))

    def total_from(p):
        return remote(total, totals.at[c, p], total_send.at[p], total_got.at[p], chip(p))

    across(lambda p: total_to(p).start())
    totals[c, me] = total[...]
    across(lambda p: total_from(p).wait_recv())
    last_swap = remote(totals.at[c], totals.at[c], last_send, last_got, pair)
    last_swap.start()
    remote(totals.at[1 - c], totals.at[1 - c], last_send, last_got, pair).wait_recv()
    grad_out[...] = totals[...].reshape(WIDE, D)

    last_swap.wait_send()
    swap.wait_send()
    along(lambda p: name_to(p).wait_send())
    along(lambda p: stat_to(p).wait_send())
    along(lambda p: note_to(p).wait_send())
    across(lambda p: piece_to(p).wait_send())
    across(lambda p: total_to(p).wait_send())

    def ring_sent(i):
        for h in range(2):
            rise(i, h).wait_send()

            @pl.when(i < 7)
            def _():
                sink(i, h).wait_send()

    loop(0, 8, ring_sent)


def run_head(hn, weight, names, meta):
    local = pl.BlockSpec(memory_space=VMEM)
    return pl.pallas_call(
        head_kernel,
        out_shape=(jax.ShapeDtypeStruct((8, 128), F32), jax.ShapeDtypeStruct((WIDE, D), BF16)),
        in_specs=[local] * 4,
        out_specs=(local, local),
        scratch_shapes=[
            VMEM((RING, 2, FRAMES, HALF), BF16),
            VMEM((RING, 8, 128), F32),
            VMEM((RING * FRAMES, WIDE), F32),
            VMEM((RING, 8, 128), F32),
            VMEM((RING, 8, 128), F32),
            VMEM((FRAMES, 128), F32),
            VMEM((FRAMES, 128), F32),
            VMEM((FRAMES, 128), F32),
            VMEM((8, 128), F32),
            VMEM((RING, 8, 128), F32),
            VMEM((RING * FRAMES, WIDE), BF16),
            VMEM((WIDE, D), F32),
            VMEM((256, D), BF16),
            VMEM((256, D), BF16),
            VMEM((RING, 16, D), BF16),
            VMEM((RING, 16, D), BF16),
            VMEM((16, D), BF16),
            VMEM((2, RING, 16, D), BF16),
            DMA((8, 2)), DMA((8, 2)), DMA((8, 2)), DMA((8, 2)),
            DMA((RING,)), DMA((RING,)), DMA((RING,)), DMA((RING,)), DMA((RING,)), DMA((RING,)),
            DMA, DMA,
            DMA((RING,)), DMA((RING,)), DMA((RING,)), DMA((RING,)),
            DMA, DMA,
        ],
        compiler_params=pltpu.CompilerParams(
            collective_id=1, has_side_effects=True, vmem_limit_bytes=VMEM_LIMIT
        ),
    )(hn, weight, names, meta)


def per_device(
    frames,
    norm_gain,
    router,
    w_in,
    w_out,
    routing,
    head_gain,
    head_weight,
    frame_lengths,
    labels,
    label_lengths,
):
    section = lax.axis_index("section")
    micro = frames.shape[0]
    mine, which = section // 2, lax.rem(section, 2)
    block = lax.dynamic_index_in_dim(frames.reshape(micro, TOK, D), mine, 0, keepdims=False)
    routes = routing[0, :, :, :, 0].reshape(micro, TOK)
    same = routes[:, :, None] == routes[:, None, :]
    earlier = jnp.arange(TOK)[:, None] < jnp.arange(TOK)[None, :]
    rank = jnp.sum((same & earlier[None]).astype(jnp.int32), axis=1)
    spots = (8 * routes + rank).astype(F32)
    spots = jnp.pad(spots, ((0, 0), (0, D - TOK)), constant_values=-1.0)
    aux = jnp.concatenate([norm_gain, spots, jnp.zeros((3, D), F32)], axis=0)
    hn = run_moe(block, w_in[0, 0], w_out[0, 0], router[0].T, aux, head_gain.reshape(1, D))

    count = labels.shape[2]
    own = lax.dynamic_index_in_dim(labels.reshape(-1, count), section, 0, keepdims=False)
    span = lax.dynamic_index_in_dim(frame_lengths.reshape(-1), section, 0, keepdims=False)
    length = lax.dynamic_index_in_dim(label_lengths.reshape(-1), section, 0, keepdims=False)
    names = jnp.concatenate([own, jnp.zeros((1,), jnp.int32), jnp.full((115,), -2, jnp.int32)]).astype(F32)
    names = jnp.broadcast_to(names[None], (8, 128))
    ext = jnp.concatenate([jnp.stack([jnp.zeros_like(own), own], axis=1).reshape(-1), jnp.zeros((1,), jnp.int32)])
    skip = jnp.concatenate([jnp.zeros((2,), bool), (ext[2:] != 0) & (ext[2:] != ext[:-2])])
    skip = jnp.pad(skip.astype(F32), (0, 128 - skip.shape[0]))
    skip_back = jnp.concatenate([skip[2:], jnp.zeros((2,), F32)])
    meta = jnp.stack(
        [jnp.full((128,), span).astype(F32), jnp.full((128,), 2 * length).astype(F32), skip, skip_back]
        + [jnp.zeros((128,), F32)] * 4
    )
    weight = jnp.pad(head_weight, ((0, 0), (0, WIDE - head_weight.shape[1])))
    losses, grad = run_head(hn, weight, names, meta)
    return losses[0:1, 0:1], grad[: head_weight.shape[1]].T


def solution(mesh):
    placed = (
        P(None, ("expert", "dp"), None, None),
        P("section", None),
        P("section", None, None),
        P("section", "expert", None, None),
        P("section", "expert", None, None),
        P("section", None, ("expert", "dp"), None, None),
        P(),
        P(None, "expert"),
        P(None, ("expert", "dp")),
        P(None, ("expert", "dp"), None),
        P(None, ("expert", "dp")),
    )
    return jax.shard_map(
        per_device,
        mesh=mesh,
        in_specs=placed,
        out_specs=(P("section", ("expert", "dp")), P(None, "expert")),
        check_vma=False,
    )
```

```python
import functools

import jax
import jax.numpy as jnp
from jax import lax
from jax.experimental import pallas as pl
from jax.experimental.pallas import tpu as pltpu
from jax.sharding import PartitionSpec as P

EPSILON = 1e-06
LOG_ZERO = -1e30
MESH = pl.DeviceIdType.MESH
F32, BF16 = jnp.float32, jnp.bfloat16
D, HALF, EFF, LAYERS, RING, TOK, FRAMES = 1280, 640, 256, 8, 16, 96, 48
PIECES = 16
SKEW = 3
TURNS = PIECES // 4
CHUNKS = LAYERS * PIECES
IN_ROWS, OUT_ROWS = D // PIECES, EFF // PIECES
SHARD, WIDE = 500, 512
PART = D // RING
HIGHEST = lax.Precision.HIGHEST
VMEM = pltpu.VMEM
DMA = pltpu.SemaphoreType.DMA
VMEM_LIMIT = 56 * 1024 * 1024


def coords():
    s, z, y = lax.axis_index("section"), lax.axis_index("expert"), lax.axis_index("dp")
    return s, s // 2, lax.rem(s, 2), z, y


def loop(low, high, body):
    def step(i, carry):
        body(i)
        return carry

    lax.fori_loop(low, high, step, 0)


def remote(src, dst, send, recv, device):
    return pltpu.make_async_remote_copy(
        src_ref=src, dst_ref=dst, send_sem=send, recv_sem=recv, device_id=device, device_id_type=MESH
    )


def dot(a, b, dims=((1,), (0,)), precision=None):
    return lax.dot_general(a, b, (dims, ((), ())), precision=precision, preferred_element_type=F32)


def rms(x, gain):
    return (x * lax.rsqrt(jnp.mean(x * x, axis=-1, keepdims=True) + EPSILON) * gain).astype(BF16)


def moe_kernel(
    frames, w_in, w_out, router, gain, routes, head_gain, hn_out,
    win, wout, aux, routers, auxes, state, give, take, answer, back, stage_in, stage_out, passed, landed,
    got_in, got_out, on_in, on_out, copy_in, copy_out, have_in, have_out,
    lay_send, stage_send, stage_got, small_send, small_got, give_send, take_got, answer_send, back_got, hn_send, hn_got, state_got,
):
    s, x, c, z, y = coords()
    me = 4 * x + y
    home_x, home_y = z // 4, lax.rem(z, 4)
    above, below = lax.rem(z + 1, RING), lax.rem(z + RING - 1, RING)
    barrier = pltpu.get_barrier_semaphore()

    def greet(i):
        p = lax.rem(4 * s + y + i, 32)
        pl.semaphore_signal(barrier, inc=1, device_id=(p // 4, z, lax.rem(p, 4)), device_id_type=MESH)

    loop(1, 32, greet)
    pl.semaphore_signal(barrier, inc=1, device_id=(s, above, y), device_id_type=MESH)
    pl.semaphore_signal(barrier, inc=1, device_id=(s, below, y), device_id_type=MESH)
    pl.semaphore_wait(barrier, 33)

    def in_rows(j):
        return pl.ds(pl.multiple_of(j * IN_ROWS, 16), IN_ROWS)

    def out_rows(j):
        return pl.ds(pl.multiple_of(j * OUT_ROWS, 16), OUT_ROWS)

    def share(layer, i, src_in, src_out):
        j = y + 4 * i
        k = layer * PIECES + j
        target = (2 * home_x + 1, z, home_y)
        return (
            remote(src_in, win.at[layer, in_rows(j)], lay_send.at[2 * c, i], got_in.at[k], target),
            remote(src_out, wout.at[layer, out_rows(j)], lay_send.at[2 * c + 1, i], got_out.at[k], target),
        )

    def staged(i):
        j = y + 4 * i
        target = (s + 1, z, y)
        return (
            remote(w_in.at[in_rows(j)], stage_in.at[i], stage_send.at[0, i], stage_got.at[0, i], target),
            remote(w_out.at[out_rows(j)], stage_out.at[i], stage_send.at[1, i], stage_got.at[1, i], target),
        )

    def small(to_x):
        target = (2 * to_x, z, y)
        return (
            remote(aux, auxes.at[s], small_send.at[0, to_x], small_got.at[0, s], target),
            remote(router, routers.at[s], small_send.at[1, to_x], small_got.at[1, s], target),
        )

    def each(copies, act):
        for copy in copies:
            act(copy)

    start, sent, got = (lambda d: d.start()), (lambda d: d.wait_send()), (lambda d: d.wait_recv())

    @pl.when((c == 0) & (x == 0))
    def _():
        for i in range(TURNS):
            each(share(0, i, w_in.at[in_rows(y + 4 * i)], w_out.at[out_rows(y + 4 * i)]), start)

    @pl.when((c == 0) & (x > 0))
    def _():
        for i in range(TURNS):
            each(staged(i), start)

    rows, cols = lax.broadcasted_iota(jnp.int32, (128, 128), 0), lax.broadcasted_iota(jnp.int32, (128, 128), 1)
    aux[...] = jnp.zeros_like(aux)
    aux[0:1, :] = gain[...]
    for m in range(4):
        named = jnp.broadcast_to(routes[m : m + 1, :], (128, 128))
        before = (jnp.transpose(named) == named) & (rows < cols)
        rank = jnp.sum(before.astype(F32), axis=0, keepdims=True)
        live = lax.broadcasted_iota(jnp.int32, (1, 128), 1) < TOK
        aux[m + 1 : m + 2, 0:128] = jnp.where(live, 8.0 * routes[m : m + 1, :] + rank, -1.0)

    for gap in range(1, 4):
        each(small(lax.rem(x + gap, 4)), start)

    own_small = (
        pltpu.make_async_copy(aux, auxes.at[s], small_got.at[0, s]),
        pltpu.make_async_copy(router, routers.at[s], small_got.at[1, s]),
    )

    @pl.when(c == 1)
    def _():
        each(small(x), start)

    @pl.when(c == 0)
    def _():
        each(own_small, start)

    @pl.when(c == 1)
    def _():
        at_home = (x == home_x) & (y == home_y)
        up, down = lax.rem(z + RING - me, RING), lax.rem(me + RING - z, RING)

        def distribute(layer, slot, pick):
            for i in range(TURNS):
                j = y + 4 * i
                src_in, src_out = pick(i)

                @pl.when(at_home)
                def _():
                    k = layer * PIECES + j
                    pltpu.make_async_copy(src_in, win.at[layer, in_rows(j)], got_in.at[k]).start()
                    pltpu.make_async_copy(src_out, wout.at[layer, out_rows(j)], got_out.at[k]).start()

                @pl.when(jnp.logical_not(at_home))
                def _():
                    each(carried(layer, slot, i, src_in, src_out), start)

        def carried(layer, slot, i, src_in, src_out):
            j = y + 4 * i
            k = layer * PIECES + j
            target = (2 * home_x + 1, z, home_y)
            return (
                remote(src_in, win.at[layer, in_rows(j)], lay_send.at[2 * slot, i], got_in.at[k], target),
                remote(src_out, wout.at[layer, out_rows(j)], lay_send.at[2 * slot + 1, i], got_out.at[k], target),
            )

        def from_stage(i):
            return stage_in.at[i], stage_out.at[i]

        def from_own(i):
            return w_in.at[in_rows(y + 4 * i)], w_out.at[out_rows(y + 4 * i)]

        def rise(k):
            layer, j = k // PIECES, lax.rem(k, PIECES)
            ref = win.at[layer, in_rows(j)]
            return remote(ref, ref, on_in, got_in.at[k], (s, above, y))

        def sink(k):
            layer, j = k // PIECES, lax.rem(k, PIECES)
            ref = wout.at[layer, out_rows(j)]
            return remote(ref, ref, on_out, got_out.at[k], (s, below, y))

        def hand_in(layer):
            return remote(win.at[layer], win.at[layer], copy_in.at[layer], have_in.at[layer], (s - 1, z, y))

        def hand_out(layer):
            return remote(wout.at[layer], wout.at[layer], copy_out.at[layer], have_out.at[layer], (s - 1, z, y))

        def tick(t):
            @pl.when((x > 0) & (t == PIECES * (2 * x - 1)))
            def _():
                for i in range(TURNS):
                    each(staged(i), got)
                distribute(2 * x, 0, from_stage)

            @pl.when(t == 2 * PIECES * x)
            def _():
                distribute(2 * x + 1, 1, from_own)

            ku, kd = t - SKEW * up, t - SKEW * down

            @pl.when((ku >= 0) & (ku < CHUNKS))
            def _():
                rise(ku).wait_recv()

                @pl.when(up < RING - 1)
                def _():
                    rise(ku).start()

                @pl.when(lax.rem(ku, PIECES) == PIECES - 1)
                def _():
                    hand_in(ku // PIECES).start()

            @pl.when((kd >= 0) & (kd < CHUNKS))
            def _():
                sink(kd).wait_recv()

                @pl.when(down < RING - 1)
                def _():
                    sink(kd).start()

                @pl.when(lax.rem(kd, PIECES) == PIECES - 1)
                def _():
                    hand_out(kd // PIECES).start()

        loop(0, CHUNKS + SKEW * (RING - 1), tick)

        @pl.when(jnp.logical_not(at_home))
        def _():
            for i in range(TURNS):
                @pl.when(x > 0)
                def _():
                    each(carried(2 * x, 0, i, *from_stage(i)), sent)

                each(carried(2 * x + 1, 1, i, *from_own(i)), sent)

        @pl.when(up < RING - 1)
        def _():
            pltpu.make_async_copy(win, win, on_in).wait()

        @pl.when(down < RING - 1)
        def _():
            pltpu.make_async_copy(wout, wout, on_out).wait()

        loop(0, LAYERS, lambda layer: hand_in(layer).wait_send())
        loop(0, LAYERS, lambda layer: hand_out(layer).wait_send())
        each(small(x), sent)

    @pl.when(c == 0)
    def _():
        pltpu.make_async_copy(frames.at[x], state, state_got).start()

        def smalls(layer):
            pltpu.make_async_copy(aux, auxes.at[layer], small_got.at[0, layer]).wait()
            pltpu.make_async_copy(router, routers.at[layer], small_got.at[1, layer]).wait()

        loop(0, LAYERS, smalls)
        pltpu.make_async_copy(frames.at[x], state, state_got).wait()

        def chip(p):
            return (2 * (p // 4), z, lax.rem(p, 4))

        def out_to(p):
            return remote(give.at[p], take.at[me], give_send, take_got, chip(p))

        def back_to(p):
            return remote(answer.at[p], back.at[me], answer_send, back_got, chip(p))

        def start_all(copy):
            for i in range(1, RING):
                copy(lax.rem(me + i, RING)).start()

        def wait_all(buffer, sem):
            most = buffer.at[pl.ds(0, RING - 1)]
            pltpu.make_async_copy(most, most, sem).wait()

        def layer_step(layer):
            xf = state[...].astype(F32)
            normed = rms(xf, auxes[layer, 0:1, :])
            which = lax.broadcasted_iota(jnp.int32, (8, 128), 0) == 1 + x
            spots = jnp.sum(jnp.where(which, auxes[layer, :, 0:128], 0.0), axis=0, keepdims=True)
            pick = (lax.broadcasted_iota(jnp.int32, (128, 128), 0).astype(F32) == spots)[:, :TOK]
            pick = pick.astype(F32).astype(BF16)
            left = dot(pick, normed[:, :HALF]).reshape(RING, 8, HALF)
            right = dot(pick, normed[:, HALF:]).reshape(RING, 8, HALF)
            give[...] = jnp.concatenate([left, right], axis=1).astype(BF16)
            start_all(out_to)
            take[me] = give[me]

            columns = jnp.transpose(jnp.broadcast_to(spots, (128, 128)))[:TOK, :].astype(jnp.int32)
            lane = lax.broadcasted_iota(jnp.int32, (TOK, 128), 1)
            logits = dot(normed, routers[layer], ((1,), (1,)))
            mine = (lane[:, :RING] == (columns[:, :RING] >> 3)).astype(F32)
            gate = jax.nn.sigmoid(jnp.sum(mine * logits, axis=1, keepdims=True))
            place = columns + ((columns >> 3) << 3)
            spread = [(lane + 128 * h == place + 8 * b).astype(F32).astype(BF16) for b in range(2) for h in range(2)]
            put_left = jnp.concatenate(spread[:2], axis=1)
            put_right = jnp.concatenate(spread[2:], axis=1)

            pltpu.make_async_copy(win.at[layer], win.at[layer], have_in.at[layer]).wait()
            wait_all(take, take_got)
            rows = take[...].reshape(RING * 16, HALF)
            first = dot(rows, win[layer, 0:HALF, :]).reshape(RING, 16, EFF)
            second = dot(rows, win[layer, HALF:D, :]).reshape(RING, 16, EFF)
            hidden = (first[:, 0:8] + second[:, 8:16]).reshape(128, EFF)
            active = (hidden * jax.nn.sigmoid(hidden)).astype(BF16)
            pltpu.make_async_copy(wout.at[layer], wout.at[layer], have_out.at[layer]).wait()
            result = dot(active, wout[layer]).reshape(RING, 8, D)
            answer[...] = jnp.concatenate([result[:, :, :HALF], result[:, :, HALF:]], axis=1).astype(BF16)
            start_all(back_to)
            back[me] = answer[me]
            wait_all(give, give_send)
            wait_all(back, back_got)
            returned = back[...].reshape(RING * 16, HALF)
            mixed = jnp.concatenate([dot(put_left, returned), dot(put_right, returned)], axis=1)
            state[...] = (xf + gate * mixed).astype(BF16)
            wait_all(answer, answer_send)

        loop(0, LAYERS, layer_step)
        hn = rms(state[...].astype(F32), head_gain[...])
        for h in range(2):
            hn_out[h] = hn[:FRAMES, HALF * h : HALF * (h + 1)]
            passed[h] = hn[FRAMES:, HALF * h : HALF * (h + 1)]
        remote(passed, landed, hn_send, hn_got, (s + 1, z, y)).start()

        @pl.when(x == 0)
        def _():
            for i in range(TURNS):
                each(share(0, i, w_in.at[in_rows(y + 4 * i)], w_out.at[out_rows(y + 4 * i)]), sent)

        @pl.when(x > 0)
        def _():
            for i in range(TURNS):
                each(staged(i), sent)

        remote(passed, landed, hn_send, hn_got, (s + 1, z, y)).wait_send()

    @pl.when(c == 1)
    def _():
        remote(passed, landed, hn_send, hn_got, (s, z, y)).wait_recv()
        hn_out[...] = landed[...]

    for gap in range(1, 4):
        each(small(lax.rem(x + gap, 4)), sent)


def run_moe(frames, w_in, w_out, router, gain, routes, head_gain):
    anywhere, local = pl.BlockSpec(memory_space=pl.ANY), pl.BlockSpec(memory_space=VMEM)
    return pl.pallas_call(
        moe_kernel,
        out_shape=jax.ShapeDtypeStruct((2, FRAMES, HALF), BF16),
        in_specs=[anywhere, anywhere, anywhere, local, local, local, local],
        out_specs=local,
        scratch_shapes=[
            VMEM((LAYERS, D, EFF), BF16),
            VMEM((LAYERS, EFF, D), BF16),
            VMEM((8, D), F32),
            VMEM((LAYERS, 16, D), BF16),
            VMEM((LAYERS, 8, D), F32),
            VMEM((TOK, D), BF16),
            VMEM((RING, 16, HALF), BF16),
            VMEM((RING, 16, HALF), BF16),
            VMEM((RING, 16, HALF), BF16),
            VMEM((RING, 16, HALF), BF16),
            VMEM((TURNS, IN_ROWS, EFF), BF16),
            VMEM((TURNS, OUT_ROWS, D), BF16),
            VMEM((2, FRAMES, HALF), BF16),
            VMEM((2, FRAMES, HALF), BF16),
            DMA((CHUNKS,)), DMA((CHUNKS,)), DMA, DMA,
            DMA((LAYERS,)), DMA((LAYERS,)), DMA((LAYERS,)), DMA((LAYERS,)),
            DMA((4, TURNS)), DMA((2, TURNS)), DMA((2, TURNS)), DMA((2, 4)), DMA((2, LAYERS)),
            DMA, DMA, DMA, DMA,
            DMA, DMA, DMA,
        ],
        compiler_params=pltpu.CompilerParams(
            collective_id=0, has_side_effects=True, vmem_limit_bytes=VMEM_LIMIT
        ),
    )(frames, w_in, w_out, router, gain, routes, head_gain)


def flip(block):
    rows = block.shape[0]
    if rows < 128:
        block = jnp.concatenate([block, jnp.zeros((128 - rows, 128), F32)], axis=0)
    return jnp.transpose(block)


def pack(columns):
    turned = flip(columns)
    return turned[0:8] + pltpu.roll(turned[8:16], 64, 1)


def lanes(rows):
    return lax.broadcasted_iota(jnp.int32, (rows, 128), 1)


def triple(a, b, c):
    top = jnp.maximum(jnp.maximum(a, b), c)
    return top + jnp.log(jnp.exp(a - top) + jnp.exp(b - top) + jnp.exp(c - top))


def head_kernel(
    hn, weight, numbers, loss_out, grad_out,
    rows_all, names, names_all, logits, stats, stats_all, emit, ahead, behind, notes, notes_all, grads, partial,
    half_out, half_in, pieces, pieces_all, total, totals,
    up_send, up_got, down_send, down_got, name_send, name_got, stat_send, stat_got, note_send, note_got,
    half_send, half_got, piece_send, piece_got, total_send, total_got, last_send, last_got,
):
    s, x, c, z, y = coords()
    me = 4 * x + y
    pair = (s + 1 - 2 * c, z, y)
    above, below = lax.rem(z + 1, RING), lax.rem(z + RING - 1, RING)
    barrier = pltpu.get_barrier_semaphore()

    def chip(p):
        return (2 * (p // 4) + c, z, lax.rem(p, 4))

    def greet(i):
        pl.semaphore_signal(barrier, inc=1, device_id=(s, lax.rem(z + i, RING), y), device_id_type=MESH)
        pl.semaphore_signal(barrier, inc=1, device_id=chip(lax.rem(me + i, RING)), device_id_type=MESH)

    loop(1, RING, greet)
    pl.semaphore_signal(barrier, inc=1, device_id=pair, device_id_type=MESH)
    pl.semaphore_wait(barrier, 31)

    def along(act):
        for i in range(1, RING):
            act(lax.rem(z + i, RING))

    def across(act):
        for i in range(1, RING):
            act(lax.rem(me + i, RING))

    def rise(i, h):
        block = rows_all.at[lax.rem(z + RING - i, RING), h]
        return remote(block, block, up_send.at[i, h], up_got.at[i, h], (s, above, y))

    def sink(i, h):
        block = rows_all.at[lax.rem(z + i, RING), h]
        return remote(block, block, down_send.at[i, h], down_got.at[i, h], (s, below, y))

    def risen(i, h):
        block = rows_all.at[lax.rem(z + RING - i, RING), h]
        return remote(block, block, up_send.at[i - 1, h], up_got.at[i - 1, h], (s, above, y))

    def sunk(i, h):
        block = rows_all.at[lax.rem(z + i, RING), h]
        return remote(block, block, down_send.at[i - 1, h], down_got.at[i - 1, h], (s, below, y))

    rows_all[z] = hn[...]
    for h in range(2):
        rise(0, h).start()
        sink(0, h).start()

    one = lanes(1)
    chosen = lax.broadcasted_iota(jnp.int32, (8, 128), 0) == s
    known_row = jnp.sum(jnp.where(chosen, numbers[...], 0.0), axis=0, keepdims=True)
    tags = jnp.where(one < 12, known_row, jnp.where(one == 12, 0.0, -2.0))
    names[...] = jnp.broadcast_to(tags, (8, 128))

    def all_but_one(buffer, sem):
        most = buffer.at[pl.ds(0, RING - 1)]
        pltpu.make_async_copy(most, most, sem).wait()

    def name_to(p):
        return remote(names, names_all.at[z], name_send, name_got, (s, p, y))

    along(lambda p: name_to(p).start())
    names_all[z] = names[...]
    logits[:, WIDE - 128 : WIDE] = jnp.zeros((RING * FRAMES, 128), F32)

    columns = lax.broadcasted_iota(jnp.int32, (128, WIDE), 1)
    valid = columns[:FRAMES] < SHARD
    owned = jnp.where(columns < SHARD, columns + SHARD * z, -1).astype(F32)

    def selector(k):
        wanted = flip(jnp.broadcast_to(names_all[k, 0:1, :], (128, 128)))
        return (jnp.concatenate([wanted] * 4, axis=1) == owned).astype(F32).astype(BF16)

    def thirds(value):
        high = value.astype(BF16)
        rest = value - high.astype(F32)
        middle = rest.astype(BF16)
        return jnp.concatenate([high, middle, (rest - middle.astype(F32)).astype(BF16)], axis=0)

    def joined(parts):
        return parts[0:FRAMES] + parts[FRAMES : 2 * FRAMES] + parts[2 * FRAMES :]

    def frames_of(k):
        return pl.ds(pl.multiple_of(k * FRAMES, FRAMES), FRAMES)

    lane = lanes(FRAMES)

    def stat_to(p):
        return remote(stats.at[p], stats_all.at[z], stat_send, stat_got, (s, p, y))

    def evaluate(blocks):
        def side(h):
            return jnp.concatenate([rows_all[k, h] for k in blocks], axis=0)

        value = dot(side(0), weight[0:HALF, :]) + dot(side(1), weight[HALF:D, :])
        for n, k in enumerate(blocks):
            logits[frames_of(k), 0:SHARD] = value[n * FRAMES : (n + 1) * FRAMES]
        for k in blocks:
            block = logits[frames_of(k), :]
            peak = jnp.max(jnp.where(valid, block, -jnp.inf), axis=1, keepdims=True)
            weightsum = jnp.sum(jnp.where(valid, jnp.exp(block - peak), 0.0), axis=1, keepdims=True)
            found = joined(dot(thirds(block), selector(k), ((1,), (1,))))
            stats[k] = pack(jnp.where(lane == 13, peak, jnp.where(lane == 14, weightsum, found)))

    def ring_step(i):
        for h in range(2):
            risen(i, h).wait_recv()

            @pl.when(i < 8)
            def _():
                rise(i, h).start()
                sunk(i, h).wait_recv()

            @pl.when(i < 7)
            def _():
                sink(i, h).start()

        @pl.when(i == 1)
        def _():
            all_but_one(names_all, name_got)

        lower, upper = lax.rem(z + RING + 1 - i, RING), lax.rem(z + i - 1, RING)
        evaluate((lower, upper))

        @pl.when(i > 1)
        def _():
            stat_to(lower).start()
            stat_to(upper).start()

    loop(1, 9, ring_step)
    opposite = lax.rem(z + 8, RING)
    evaluate((opposite,))
    stat_to(opposite).start()
    stats_all[z] = stats[z]
    all_but_one(stats_all, stat_got)

    low = [stats_all[k] for k in range(RING)]
    high = [pltpu.roll(v, 64, 1) for v in low]
    peaks = functools.reduce(jnp.maximum, high)
    sums = sum(v * pltpu.roll(jnp.exp(v - peaks), 1, 0) for v in high)
    live = lanes(1) < FRAMES
    log_total = jnp.where(live, peaks[5:6] + jnp.log(jnp.where(live, sums[6:7], 1.0)), 0.0)
    both = jnp.concatenate([sum(low), sum(high)], axis=0)
    slot = lax.broadcasted_iota(jnp.int32, (16, 128), 0)
    both = jnp.where(lanes(16) < FRAMES, both - log_total, 0.0)
    both = jnp.where(slot < 13, both, jnp.where(slot == 14, log_total, 0.0))
    by_label = flip(both)
    row, col = lax.broadcasted_iota(jnp.int32, (128, 128), 0), lanes(128)
    odd = (col & 1) == 1
    expand = (col < 25) & (jnp.where(odd, col >> 1, 12) == row)
    expand = expand.astype(F32)
    emit[...] = dot(by_label[:FRAMES], expand, precision=HIGHEST)
    total_col = by_label[:FRAMES]
    span = jnp.sum(jnp.where(one == 12, known_row, 0.0), axis=1, keepdims=True)
    last = 2.0 * jnp.sum(jnp.where(one == 13, known_row, 0.0), axis=1, keepdims=True)
    differs = (known_row != pltpu.roll(known_row, 1, 1)) & (known_row != 0.0) & (one > 0) & (one < 12)
    jumps = dot(jnp.broadcast_to(differs.astype(F32), (8, 128)), expand)[0:1]
    jump, jump_back = jumps > 0.5, pltpu.roll(jumps, 126, 1) > 0.5
    spot = one.astype(F32)
    ends = (spot == last) | (spot == last - 1.0)
    closing = jnp.where(ends, 0.0, LOG_ZERO)
    opening = jnp.where(one < 2, emit[0:1, :], LOG_ZERO)
    ahead[0:1, :] = opening
    behind[FRAMES - 1 : FRAMES, :] = closing

    def ctc_step(i, carry):
        a, b = carry
        once = jnp.where(one < 1, LOG_ZERO, pltpu.roll(a, 1, 1))
        twice = jnp.where(jump, pltpu.roll(a, 2, 1), LOG_ZERO)
        moved = triple(a, once, twice) + emit[pl.ds(i, 1), :]
        a = jnp.where(i.astype(F32) < span, moved, a)
        ahead[pl.ds(i, 1), :] = a
        t = FRAMES - 1 - i
        g = b + emit[pl.ds(t + 1, 1), :]
        once = jnp.where(one > 126, LOG_ZERO, pltpu.roll(g, 127, 1))
        twice = jnp.where(jump_back, pltpu.roll(g, 126, 1), LOG_ZERO)
        b = jnp.where(t.astype(F32) < span - 1.0, triple(g, once, twice), closing)
        behind[pl.ds(t, 1), :] = b
        return a, b

    final, _ = lax.fori_loop(1, FRAMES, ctc_step, (opening, closing))
    tail = jnp.where(ends, final, LOG_ZERO)
    top = jnp.max(tail, axis=1, keepdims=True)
    likely = top + jnp.log(jnp.sum(jnp.where(ends, jnp.exp(final - top), 0.0), axis=1, keepdims=True))
    loss_out[...] = jnp.broadcast_to(-likely, (8, 128))
    when = lax.broadcasted_iota(jnp.int32, (FRAMES, 128), 0).astype(F32)
    occupied = jnp.where(
        (when < span) & (lane < 25), -jnp.exp(ahead[...] + behind[...] - likely), 0.0
    )
    merged = dot(occupied, expand, ((1,), (1,)), HIGHEST)
    mass = jnp.sum(occupied, axis=1, keepdims=True)
    notes[...] = pack(
        jnp.where(lane == 13, mass, jnp.where(lane == 14, total_col, jnp.where(lane < 13, merged, 0.0)))
    )
    notes_all[z] = notes[...]

    def note_to(p):
        return remote(notes, notes_all.at[z], note_send, note_got, (s, p, y))

    along(lambda p: note_to(p).start())
    all_but_one(notes_all, note_got)

    def spread(pair_at):
        for k in (2 * pair_at, 2 * pair_at + 1):
            packed = notes_all[k]
            known = flip(jnp.concatenate([packed, pltpu.roll(packed, 64, 1)], axis=0))[:FRAMES]
            scattered = joined(dot(thirds(known), selector(k)))
            block = logits[frames_of(k), :]
            value = scattered - jnp.exp(block - known[:, 14:15]) * known[:, 13:14]
            grads[frames_of(k), :] = jnp.where(valid, value, 0.0).astype(BF16)

    loop(0, RING // 2, spread)
    for h in range(2):
        partial[HALF * h : HALF * (h + 1), :] = dot(
            rows_all[:, h].reshape(RING * FRAMES, HALF), grads[...], ((0,), (0,))
        )

    def mine(core):
        return pl.ds(pl.multiple_of(256 * core, 256), 256)

    half_out[...] = partial[:, mine(1 - c)].astype(BF16)
    swap = remote(half_out, half_in, half_send, half_got, pair)
    swap.start()
    swap.wait_recv()
    pieces[...] = (partial[:, mine(c)] + half_in[...].astype(F32)).astype(BF16).reshape(RING, PART, 256)

    def piece_to(p):
        return remote(pieces.at[p], pieces_all.at[me], piece_send, piece_got, chip(p))

    across(lambda p: piece_to(p).start())
    pieces_all[me] = pieces[me]
    all_but_one(pieces_all, piece_got)
    total[...] = sum(pieces_all[k].astype(F32) for k in range(RING)).astype(BF16)

    def total_to(p):
        return remote(total, totals.at[c, me], total_send, total_got, chip(p))

    across(lambda p: total_to(p).start())
    totals[c, me] = total[...]
    all_but_one(totals.at[c], total_got)
    last_swap = remote(totals.at[c], totals.at[c], last_send, last_got, pair)
    last_swap.start()
    remote(totals.at[1 - c], totals.at[1 - c], last_send, last_got, pair).wait_recv()
    grad_out[:, 0:256] = totals[0].reshape(D, 256)
    grad_out[:, 256:SHARD] = totals[1].reshape(D, 256)[:, : SHARD - 256]

    last_swap.wait_send()
    swap.wait_send()
    all_but_one(names_all, name_send)
    all_but_one(stats, stat_send)
    all_but_one(notes_all, note_send)
    all_but_one(pieces, piece_send)
    all_but_one(pieces, total_send)

    def ring_sent(i):
        for h in range(2):
            rise(i, h).wait_send()

            @pl.when(i < 7)
            def _():
                sink(i, h).wait_send()

    loop(0, 8, ring_sent)


def run_head(hn, weight, numbers):
    local = pl.BlockSpec(memory_space=VMEM)
    return pl.pallas_call(
        head_kernel,
        out_shape=(jax.ShapeDtypeStruct((8, 128), F32), jax.ShapeDtypeStruct((D, SHARD), BF16)),
        in_specs=[local] * 3,
        out_specs=(local, local),
        scratch_shapes=[
            VMEM((RING, 2, FRAMES, HALF), BF16),
            VMEM((8, 128), F32),
            VMEM((RING, 8, 128), F32),
            VMEM((RING * FRAMES, WIDE), F32),
            VMEM((RING, 8, 128), F32),
            VMEM((RING, 8, 128), F32),
            VMEM((FRAMES, 128), F32),
            VMEM((FRAMES, 128), F32),
            VMEM((FRAMES, 128), F32),
            VMEM((8, 128), F32),
            VMEM((RING, 8, 128), F32),
            VMEM((RING * FRAMES, WIDE), BF16),
            VMEM((D, WIDE), F32),
            VMEM((D, 256), BF16),
            VMEM((D, 256), BF16),
            VMEM((RING, PART, 256), BF16),
            VMEM((RING, PART, 256), BF16),
            VMEM((PART, 256), BF16),
            VMEM((2, RING, PART, 256), BF16),
            DMA((8, 2)), DMA((8, 2)), DMA((8, 2)), DMA((8, 2)),
            DMA, DMA, DMA, DMA, DMA, DMA,
            DMA, DMA,
            DMA, DMA, DMA, DMA,
            DMA, DMA,
        ],
        compiler_params=pltpu.CompilerParams(
            collective_id=1, has_side_effects=True, vmem_limit_bytes=VMEM_LIMIT
        ),
    )(hn, weight, numbers)


def per_device(
    frames,
    norm_gain,
    router,
    w_in,
    w_out,
    routing,
    head_gain,
    head_weight,
    frame_lengths,
    labels,
    label_lengths,
):
    micro = frames.shape[0]
    routes = routing[0, :, :, :, 0].reshape(micro, TOK).astype(F32)
    routes = jnp.pad(routes, ((0, 8 - micro), (0, 128 - TOK)), constant_values=-1.0)
    hn = run_moe(
        frames.reshape(micro, TOK, D), w_in[0, 0], w_out[0, 0], router[0].T, norm_gain, routes, head_gain.reshape(1, D)
    )
    pairs, count = 2 * micro, labels.shape[2]
    numbers = jnp.concatenate(
        [labels.reshape(pairs, count), frame_lengths.reshape(pairs, 1), label_lengths.reshape(pairs, 1)], axis=1
    )
    numbers = jnp.pad(numbers.astype(F32), ((0, 0), (0, 128 - numbers.shape[1])))
    losses, grad = run_head(hn, head_weight, numbers)
    return losses[0:1, 0:1], grad


def solution(mesh):
    placed = (
        P(None, ("expert", "dp"), None, None),
        P("section", None),
        P("section", None, None),
        P("section", "expert", None, None),
        P("section", "expert", None, None),
        P("section", None, ("expert", "dp"), None, None),
        P(),
        P(None, "expert"),
        P(None, ("expert", "dp")),
        P(None, ("expert", "dp"), None),
        P(None, ("expert", "dp")),
    )
    return jax.shard_map(
        per_device,
        mesh=mesh,
        in_specs=placed,
        out_specs=(P("section", ("expert", "dp")), P(None, "expert")),
        check_vma=False,
    )
```

```python
import functools

import jax
import jax.numpy as jnp
from jax import lax
from jax.experimental import pallas as pl
from jax.experimental.pallas import tpu as pltpu
from jax.sharding import PartitionSpec as P

EPSILON = 1e-06
LOG_ZERO = -1e30
MESH = pl.DeviceIdType.MESH
F32, BF16 = jnp.float32, jnp.bfloat16
D, HALF, EFF, LAYERS, RING, TOK, FRAMES = 1280, 640, 256, 8, 16, 96, 48
PIECES = 16
SKEW = 4
TURNS = PIECES // 4
CHUNKS = LAYERS * PIECES
IN_ROWS, OUT_ROWS = D // PIECES, EFF // PIECES
SHARD, WIDE = 500, 512
PART = D // RING
HIGHEST = lax.Precision.HIGHEST
VMEM = pltpu.VMEM
DMA = pltpu.SemaphoreType.DMA
VMEM_LIMIT = 56 * 1024 * 1024
PLANE = sorted([(a, b) for a in range(4) for b in range(4) if a or b], key=lambda d: -sum(min(v, 4 - v) for v in d))
AROUND = sorted(range(1, RING), key=lambda d: -min(d, RING - d))


def coords():
    s, z, y = lax.axis_index("section"), lax.axis_index("expert"), lax.axis_index("dp")
    return s, s // 2, lax.rem(s, 2), z, y


def loop(low, high, body):
    def step(i, carry):
        body(i)
        return carry

    lax.fori_loop(low, high, step, 0)


def remote(src, dst, send, recv, device):
    return pltpu.make_async_remote_copy(
        src_ref=src, dst_ref=dst, send_sem=send, recv_sem=recv, device_id=device, device_id_type=MESH
    )


def dot(a, b, dims=((1,), (0,)), precision=None):
    return lax.dot_general(a, b, (dims, ((), ())), precision=precision, preferred_element_type=F32)


def rms(x, gain):
    return (x * lax.rsqrt(jnp.mean(x * x, axis=-1, keepdims=True) + EPSILON) * gain).astype(BF16)


def moe_kernel(
    frames, w_in, w_out, router, gain, routes, head_gain, hn_out,
    win, wout, aux, routers, auxes, state, give, take, answer, back, stage_in, stage_out, passed, landed,
    got_in, got_out, on_in, on_out, copy_in, copy_out, have_in, have_out,
    lay_send, stage_send, stage_got, small_send, small_got, give_send, take_got, answer_send, back_got, hn_send, hn_got, state_got,
):
    s, x, c, z, y = coords()
    me = 4 * x + y
    home_x, home_y = z // 4, lax.rem(z, 4)
    above, below = lax.rem(z + 1, RING), lax.rem(z + RING - 1, RING)
    barrier = pltpu.get_barrier_semaphore()

    def greet(i):
        p = lax.rem(4 * s + y + i, 32)
        pl.semaphore_signal(barrier, inc=1, device_id=(p // 4, z, lax.rem(p, 4)), device_id_type=MESH)

    loop(1, 32, greet)

    def greet_ring(i):
        pl.semaphore_signal(barrier, inc=1, device_id=(s, lax.rem(z + i, RING), y), device_id_type=MESH)

    loop(1, RING, greet_ring)
    pl.semaphore_wait(barrier, 46)

    def in_rows(j):
        return pl.ds(pl.multiple_of(j * IN_ROWS, 16), IN_ROWS)

    def out_rows(j):
        return pl.ds(pl.multiple_of(j * OUT_ROWS, 16), OUT_ROWS)

    def share(layer, i, src_in, src_out):
        j = y + 4 * i
        k = layer * PIECES + j
        target = (2 * home_x + 1, z, home_y)
        return (
            remote(src_in, win.at[layer, in_rows(j)], lay_send.at[2 * c, i], got_in.at[k], target),
            remote(src_out, wout.at[layer, out_rows(j)], lay_send.at[2 * c + 1, i], got_out.at[k], target),
        )

    def staged(i):
        j = y + 4 * i
        target = (s + 1, z, y)
        return (
            remote(w_in.at[in_rows(j)], stage_in.at[i], stage_send.at[0, i], stage_got.at[0, i], target),
            remote(w_out.at[out_rows(j)], stage_out.at[i], stage_send.at[1, i], stage_got.at[1, i], target),
        )

    def small(to_x):
        target = (2 * to_x, z, y)
        return (
            remote(aux, auxes.at[s], small_send.at[0, to_x], small_got.at[0, s], target),
            remote(router, routers.at[s], small_send.at[1, to_x], small_got.at[1, s], target),
        )

    def each(copies, act):
        for copy in copies:
            act(copy)

    start, sent, got = (lambda d: d.start()), (lambda d: d.wait_send()), (lambda d: d.wait_recv())

    @pl.when((c == 0) & (x == 0))
    def _():
        for i in range(TURNS):
            each(share(0, i, w_in.at[in_rows(y + 4 * i)], w_out.at[out_rows(y + 4 * i)]), start)

    @pl.when((c == 0) & (x > 0))
    def _():
        for i in range(TURNS):
            each(staged(i), start)

    rows, cols = lax.broadcasted_iota(jnp.int32, (128, 128), 0), lax.broadcasted_iota(jnp.int32, (128, 128), 1)
    aux[...] = jnp.zeros_like(aux)
    aux[0:1, :] = gain[...]
    for m in range(4):
        named = jnp.broadcast_to(routes[m : m + 1, :], (128, 128))
        before = (jnp.transpose(named) == named) & (rows < cols)
        rank = jnp.sum(before.astype(F32), axis=0, keepdims=True)
        live = lax.broadcasted_iota(jnp.int32, (1, 128), 1) < TOK
        aux[m + 1 : m + 2, 0:128] = jnp.where(live, 8.0 * routes[m : m + 1, :] + rank, -1.0)

    for gap in range(1, 4):
        each(small(lax.rem(x + gap, 4)), start)

    own_small = (
        pltpu.make_async_copy(aux, auxes.at[s], small_got.at[0, s]),
        pltpu.make_async_copy(router, routers.at[s], small_got.at[1, s]),
    )

    @pl.when(c == 1)
    def _():
        each(small(x), start)

    @pl.when(c == 0)
    def _():
        each(own_small, start)

    @pl.when(c == 1)
    def _():
        at_home = (x == home_x) & (y == home_y)
        up, down = lax.rem(z + RING - me, RING), lax.rem(me + RING - z, RING)

        def distribute(layer, slot, pick):
            for i in range(TURNS):
                j = y + 4 * i
                src_in, src_out = pick(i)

                @pl.when(at_home)
                def _():
                    k = layer * PIECES + j
                    pltpu.make_async_copy(src_in, win.at[layer, in_rows(j)], got_in.at[k]).start()
                    pltpu.make_async_copy(src_out, wout.at[layer, out_rows(j)], got_out.at[k]).start()

                @pl.when(jnp.logical_not(at_home))
                def _():
                    each(carried(layer, slot, i, src_in, src_out), start)

        def carried(layer, slot, i, src_in, src_out):
            j = y + 4 * i
            k = layer * PIECES + j
            target = (2 * home_x + 1, z, home_y)
            return (
                remote(src_in, win.at[layer, in_rows(j)], lay_send.at[2 * slot, i], got_in.at[k], target),
                remote(src_out, wout.at[layer, out_rows(j)], lay_send.at[2 * slot + 1, i], got_out.at[k], target),
            )

        def from_stage(i):
            return stage_in.at[i], stage_out.at[i]

        def from_own(i):
            return w_in.at[in_rows(y + 4 * i)], w_out.at[out_rows(y + 4 * i)]

        def rise(k):
            layer, j = k // PIECES, lax.rem(k, PIECES)
            ref = win.at[layer, in_rows(j)]
            return remote(ref, ref, on_in, got_in.at[k], (s, above, y))

        def sink(k):
            layer, j = k // PIECES, lax.rem(k, PIECES)
            ref = wout.at[layer, out_rows(j)]
            return remote(ref, ref, on_out, got_out.at[k], (s, below, y))

        def hand_in(layer):
            return remote(win.at[layer], win.at[layer], copy_in.at[layer], have_in.at[layer], (s - 1, z, y))

        def hand_out(layer):
            return remote(wout.at[layer], wout.at[layer], copy_out.at[layer], have_out.at[layer], (s - 1, z, y))

        def tick(t):
            @pl.when((x > 0) & (t == PIECES * (2 * x - 1)))
            def _():
                for i in range(TURNS):
                    each(staged(i), got)
                distribute(2 * x, 0, from_stage)

            @pl.when(t == 2 * PIECES * x)
            def _():
                distribute(2 * x + 1, 1, from_own)

            ku, kd = t - SKEW * up, t - SKEW * down

            @pl.when((ku >= 0) & (ku < CHUNKS))
            def _():
                rise(ku).wait_recv()

                @pl.when(up < RING - 1)
                def _():
                    rise(ku).start()

                @pl.when(lax.rem(ku, PIECES) == PIECES - 1)
                def _():
                    hand_in(ku // PIECES).start()

            @pl.when((kd >= 0) & (kd < CHUNKS))
            def _():
                sink(kd).wait_recv()

                @pl.when(down < RING - 1)
                def _():
                    sink(kd).start()

                @pl.when(lax.rem(kd, PIECES) == PIECES - 1)
                def _():
                    hand_out(kd // PIECES).start()

        loop(0, CHUNKS + SKEW * (RING - 1), tick)

        @pl.when(jnp.logical_not(at_home))
        def _():
            for i in range(TURNS):
                @pl.when(x > 0)
                def _():
                    each(carried(2 * x, 0, i, *from_stage(i)), sent)

                each(carried(2 * x + 1, 1, i, *from_own(i)), sent)

        @pl.when(up < RING - 1)
        def _():
            pltpu.make_async_copy(win, win, on_in).wait()

        @pl.when(down < RING - 1)
        def _():
            pltpu.make_async_copy(wout, wout, on_out).wait()

        loop(0, LAYERS, lambda layer: hand_in(layer).wait_send())
        loop(0, LAYERS, lambda layer: hand_out(layer).wait_send())
        each(small(x), sent)

    @pl.when(c == 0)
    def _():
        pltpu.make_async_copy(frames.at[x], state, state_got).start()

        def smalls(layer):
            pltpu.make_async_copy(aux, auxes.at[layer], small_got.at[0, layer]).wait()
            pltpu.make_async_copy(router, routers.at[layer], small_got.at[1, layer]).wait()

        loop(0, LAYERS, smalls)
        pltpu.make_async_copy(frames.at[x], state, state_got).wait()

        def chip(p):
            return (2 * (p // 4), z, lax.rem(p, 4))

        def out_to(p):
            return remote(give.at[p], take.at[me], give_send, take_got, chip(p))

        def back_to(p):
            return remote(answer.at[p], back.at[me], answer_send, back_got, chip(p))

        def start_all(copy):
            for i in range(1, RING):
                copy(lax.rem(me + i, RING)).start()

        def wait_all(buffer, sem):
            most = buffer.at[pl.ds(0, RING - 1)]
            pltpu.make_async_copy(most, most, sem).wait()

        def layer_step(layer):
            xf = state[...].astype(F32)
            normed = rms(xf, auxes[layer, 0:1, :])
            which = lax.broadcasted_iota(jnp.int32, (8, 128), 0) == 1 + x
            spots = jnp.sum(jnp.where(which, auxes[layer, :, 0:128], 0.0), axis=0, keepdims=True)
            pick = (lax.broadcasted_iota(jnp.int32, (128, 128), 0).astype(F32) == spots)[:, :TOK]
            pick = pick.astype(F32).astype(BF16)
            left = dot(pick, normed[:, :HALF]).reshape(RING, 8, HALF)
            right = dot(pick, normed[:, HALF:]).reshape(RING, 8, HALF)
            give[...] = jnp.concatenate([left, right], axis=1).astype(BF16)
            start_all(out_to)
            take[me] = give[me]

            columns = jnp.transpose(jnp.broadcast_to(spots, (128, 128)))[:TOK, :].astype(jnp.int32)
            lane = lax.broadcasted_iota(jnp.int32, (TOK, 128), 1)
            logits = dot(normed, routers[layer], ((1,), (1,)))
            mine = (lane[:, :RING] == (columns[:, :RING] >> 3)).astype(F32)
            gate = jax.nn.sigmoid(jnp.sum(mine * logits, axis=1, keepdims=True))
            place = columns + ((columns >> 3) << 3)
            spread = [(lane + 128 * h == place + 8 * b).astype(F32).astype(BF16) for b in range(2) for h in range(2)]
            put_left = jnp.concatenate(spread[:2], axis=1)
            put_right = jnp.concatenate(spread[2:], axis=1)

            pltpu.make_async_copy(win.at[layer], win.at[layer], have_in.at[layer]).wait()
            wait_all(take, take_got)
            rows = take[...].reshape(RING * 16, HALF)
            first = dot(rows, win[layer, 0:HALF, :]).reshape(RING, 16, EFF)
            second = dot(rows, win[layer, HALF:D, :]).reshape(RING, 16, EFF)
            hidden = (first[:, 0:8] + second[:, 8:16]).reshape(128, EFF)
            active = (hidden * jax.nn.sigmoid(hidden)).astype(BF16)
            pltpu.make_async_copy(wout.at[layer], wout.at[layer], have_out.at[layer]).wait()
            result = dot(active, wout[layer]).reshape(RING, 8, D)
            answer[...] = jnp.concatenate([result[:, :, :HALF], result[:, :, HALF:]], axis=1).astype(BF16)
            start_all(back_to)
            back[me] = answer[me]
            wait_all(give, give_send)
            wait_all(back, back_got)
            returned = back[...].reshape(RING * 16, HALF)
            mixed = jnp.concatenate([dot(put_left, returned), dot(put_right, returned)], axis=1)
            state[...] = (xf + gate * mixed).astype(BF16)
            wait_all(answer, answer_send)

        loop(0, LAYERS, layer_step)
        hn = rms(state[...].astype(F32), head_gain[...])
        for h in range(2):
            hn_out[h] = hn[:FRAMES, HALF * h : HALF * (h + 1)]
            passed[h] = hn[FRAMES:, HALF * h : HALF * (h + 1)]
        remote(passed, landed, hn_send, hn_got, (s + 1, z, y)).start()

        @pl.when(x == 0)
        def _():
            for i in range(TURNS):
                each(share(0, i, w_in.at[in_rows(y + 4 * i)], w_out.at[out_rows(y + 4 * i)]), sent)

        @pl.when(x > 0)
        def _():
            for i in range(TURNS):
                each(staged(i), sent)

        remote(passed, landed, hn_send, hn_got, (s + 1, z, y)).wait_send()

    @pl.when(c == 1)
    def _():
        remote(passed, landed, hn_send, hn_got, (s, z, y)).wait_recv()
        hn_out[...] = landed[...]

    for gap in range(1, 4):
        each(small(lax.rem(x + gap, 4)), sent)


def flip(block):
    rows = block.shape[0]
    if rows < 128:
        block = jnp.concatenate([block, jnp.zeros((128 - rows, 128), F32)], axis=0)
    return jnp.transpose(block)


def pack(columns):
    turned = flip(columns)
    return turned[0:8] + pltpu.roll(turned[8:16], 64, 1)


def lanes(rows):
    return lax.broadcasted_iota(jnp.int32, (rows, 128), 1)


def triple(a, b, c):
    top = jnp.maximum(jnp.maximum(a, b), c)
    return top + jnp.log(jnp.exp(a - top) + jnp.exp(b - top) + jnp.exp(c - top))


def head_kernel(
    fetch, hn, weight, numbers, loss_out, grad_out,
    rows_all, names, names_all, logits, stats, stats_all, emit, ahead, behind, notes, notes_all, grads, partial,
    half_out, half_in, pieces, pieces_all, total, totals,
    up_send, up_got, down_send, down_got, name_send, name_got, stat_send, stat_got, note_send, note_got,
    half_send, half_got, piece_send, piece_got, total_send, total_got, last_send, last_got,
):
    s, x, c, z, y = coords()
    me = 4 * x + y
    pair = (s + 1 - 2 * c, z, y)
    above, below = lax.rem(z + 1, RING), lax.rem(z + RING - 1, RING)

    def chip(p):
        return (2 * (p // 4) + c, z, lax.rem(p, 4))

    def along(act):
        for i in AROUND:
            act(lax.rem(z + i, RING))

    def across(act):
        for a, b in PLANE:
            act(4 * lax.rem(x + a, 4) + lax.rem(y + b, 4))

    def rise(i, h):
        block = rows_all.at[lax.rem(z + RING - i, RING), h]
        return remote(block, block, up_send.at[i, h], up_got.at[i, h], (s, above, y))

    def sink(i, h):
        block = rows_all.at[lax.rem(z + i, RING), h]
        return remote(block, block, down_send.at[i, h], down_got.at[i, h], (s, below, y))

    def risen(i, h):
        block = rows_all.at[lax.rem(z + RING - i, RING), h]
        return remote(block, block, up_send.at[i - 1, h], up_got.at[i - 1, h], (s, above, y))

    def sunk(i, h):
        block = rows_all.at[lax.rem(z + i, RING), h]
        return remote(block, block, down_send.at[i - 1, h], down_got.at[i - 1, h], (s, below, y))

    rows_all[z] = hn[...]
    for h in range(2):
        rise(0, h).start()
        sink(0, h).start()

    one = lanes(1)
    chosen = lax.broadcasted_iota(jnp.int32, (8, 128), 0) == s
    known_row = jnp.sum(jnp.where(chosen, numbers[...], 0.0), axis=0, keepdims=True)
    tags = jnp.where(one < 12, known_row, jnp.where(one == 12, 0.0, -2.0))
    names[...] = jnp.broadcast_to(tags, (8, 128))

    def all_but_one(buffer, sem):
        most = buffer.at[pl.ds(0, RING - 1)]
        pltpu.make_async_copy(most, most, sem).wait()

    def name_to(p):
        return remote(names, names_all.at[z], name_send, name_got, (s, p, y))

    along(lambda p: name_to(p).start())
    fetch.wait()
    names_all[z] = names[...]
    logits[:, WIDE - 128 : WIDE] = jnp.zeros((RING * FRAMES, 128), F32)

    columns = lax.broadcasted_iota(jnp.int32, (128, WIDE), 1)
    valid = columns[:FRAMES] < SHARD
    owned = jnp.where(columns < SHARD, columns + SHARD * z, -1).astype(F32)

    def selector(k):
        wanted = flip(jnp.broadcast_to(names_all[k, 0:1, :], (128, 128)))
        return (jnp.concatenate([wanted] * 4, axis=1) == owned).astype(F32).astype(BF16)

    def thirds(value):
        high = value.astype(BF16)
        rest = value - high.astype(F32)
        middle = rest.astype(BF16)
        return jnp.concatenate([high, middle, (rest - middle.astype(F32)).astype(BF16)], axis=0)

    def joined(parts):
        return parts[0:FRAMES] + parts[FRAMES : 2 * FRAMES] + parts[2 * FRAMES :]

    def frames_of(k):
        return pl.ds(pl.multiple_of(k * FRAMES, FRAMES), FRAMES)

    lane = lanes(FRAMES)

    def stat_to(p):
        return remote(stats.at[p], stats_all.at[z], stat_send, stat_got, (s, p, y))

    def evaluate(blocks):
        def side(h):
            return jnp.concatenate([rows_all[k, h] for k in blocks], axis=0)

        value = dot(side(0), weight[0:HALF, :]) + dot(side(1), weight[HALF:D, :])
        for n, k in enumerate(blocks):
            logits[frames_of(k), 0:SHARD] = value[n * FRAMES : (n + 1) * FRAMES]
        for k in blocks:
            block = logits[frames_of(k), :]
            peak = jnp.max(jnp.where(valid, block, -jnp.inf), axis=1, keepdims=True)
            weightsum = jnp.sum(jnp.where(valid, jnp.exp(block - peak), 0.0), axis=1, keepdims=True)
            found = joined(dot(thirds(block), selector(k), ((1,), (1,))))
            stats[k] = pack(jnp.where(lane == 13, peak, jnp.where(lane == 14, weightsum, found)))

    def ring_step(i):
        for h in range(2):
            risen(i, h).wait_recv()

            @pl.when(i < 8)
            def _():
                rise(i, h).start()
                sunk(i, h).wait_recv()

            @pl.when(i < 7)
            def _():
                sink(i, h).start()

        @pl.when(i == 1)
        def _():
            all_but_one(names_all, name_got)

        lower, upper = lax.rem(z + RING + 1 - i, RING), lax.rem(z + i - 1, RING)
        evaluate((lower, upper))

        @pl.when(i > 1)
        def _():
            stat_to(lower).start()
            stat_to(upper).start()

    loop(1, 9, ring_step)
    opposite = lax.rem(z + 8, RING)
    evaluate((opposite,))
    stat_to(opposite).start()
    stats_all[z] = stats[z]
    all_but_one(stats_all, stat_got)

    low = [stats_all[k] for k in range(RING)]
    high = [pltpu.roll(v, 64, 1) for v in low]
    peaks = functools.reduce(jnp.maximum, high)
    sums = sum(v * pltpu.roll(jnp.exp(v - peaks), 1, 0) for v in high)
    live = lanes(1) < FRAMES
    log_total = jnp.where(live, peaks[5:6] + jnp.log(jnp.where(live, sums[6:7], 1.0)), 0.0)
    both = jnp.concatenate([sum(low), sum(high)], axis=0)
    slot = lax.broadcasted_iota(jnp.int32, (16, 128), 0)
    both = jnp.where(lanes(16) < FRAMES, both - log_total, 0.0)
    both = jnp.where(slot < 13, both, jnp.where(slot == 14, log_total, 0.0))
    by_label = flip(both)
    row, col = lax.broadcasted_iota(jnp.int32, (128, 128), 0), lanes(128)
    odd = (col & 1) == 1
    expand = (col < 25) & (jnp.where(odd, col >> 1, 12) == row)
    expand = expand.astype(F32)
    emit[...] = dot(by_label[:FRAMES], expand, precision=HIGHEST)
    total_col = by_label[:FRAMES]
    span = jnp.sum(jnp.where(one == 12, known_row, 0.0), axis=1, keepdims=True)
    last = 2.0 * jnp.sum(jnp.where(one == 13, known_row, 0.0), axis=1, keepdims=True)
    differs = (known_row != pltpu.roll(known_row, 1, 1)) & (known_row != 0.0) & (one > 0) & (one < 12)
    jumps = dot(jnp.broadcast_to(differs.astype(F32), (8, 128)), expand)[0:1]
    jump, jump_back = jumps > 0.5, pltpu.roll(jumps, 126, 1) > 0.5
    spot = one.astype(F32)
    ends = (spot == last) | (spot == last - 1.0)
    closing = jnp.where(ends, 0.0, LOG_ZERO)
    opening = jnp.where(one < 2, emit[0:1, :], LOG_ZERO)
    ahead[0:1, :] = opening
    behind[FRAMES - 1 : FRAMES, :] = closing

    def ctc_step(i, carry):
        a, b = carry
        once = jnp.where(one < 1, LOG_ZERO, pltpu.roll(a, 1, 1))
        twice = jnp.where(jump, pltpu.roll(a, 2, 1), LOG_ZERO)
        moved = triple(a, once, twice) + emit[pl.ds(i, 1), :]
        a = jnp.where(i.astype(F32) < span, moved, a)
        ahead[pl.ds(i, 1), :] = a
        t = FRAMES - 1 - i
        g = b + emit[pl.ds(t + 1, 1), :]
        once = jnp.where(one > 126, LOG_ZERO, pltpu.roll(g, 127, 1))
        twice = jnp.where(jump_back, pltpu.roll(g, 126, 1), LOG_ZERO)
        b = jnp.where(t.astype(F32) < span - 1.0, triple(g, once, twice), closing)
        behind[pl.ds(t, 1), :] = b
        return a, b

    final, _ = lax.fori_loop(1, FRAMES, ctc_step, (opening, closing))
    tail = jnp.where(ends, final, LOG_ZERO)
    top = jnp.max(tail, axis=1, keepdims=True)
    likely = top + jnp.log(jnp.sum(jnp.where(ends, jnp.exp(final - top), 0.0), axis=1, keepdims=True))
    loss_out[...] = jnp.broadcast_to(-likely, (8, 128))
    when = lax.broadcasted_iota(jnp.int32, (FRAMES, 128), 0).astype(F32)
    occupied = jnp.where(
        (when < span) & (lane < 25), -jnp.exp(ahead[...] + behind[...] - likely), 0.0
    )
    merged = dot(occupied, expand, ((1,), (1,)), HIGHEST)
    mass = jnp.sum(occupied, axis=1, keepdims=True)
    notes[...] = pack(
        jnp.where(lane == 13, mass, jnp.where(lane == 14, total_col, jnp.where(lane < 13, merged, 0.0)))
    )
    notes_all[z] = notes[...]

    def note_to(p):
        return remote(notes, notes_all.at[z], note_send, note_got, (s, p, y))

    along(lambda p: note_to(p).start())
    all_but_one(notes_all, note_got)

    def spread(pair_at):
        for k in (2 * pair_at, 2 * pair_at + 1):
            packed = notes_all[k]
            known = flip(jnp.concatenate([packed, pltpu.roll(packed, 64, 1)], axis=0))[:FRAMES]
            scattered = joined(dot(thirds(known), selector(k)))
            block = logits[frames_of(k), :]
            value = scattered - jnp.exp(block - known[:, 14:15]) * known[:, 13:14]
            grads[frames_of(k), :] = jnp.where(valid, value, 0.0).astype(BF16)

    loop(0, RING // 2, spread)
    for h in range(2):
        partial[HALF * h : HALF * (h + 1), :] = dot(
            rows_all[:, h].reshape(RING * FRAMES, HALF), grads[...], ((0,), (0,))
        )

    def mine(core):
        return pl.ds(pl.multiple_of(256 * core, 256), 256)

    half_out[...] = partial[:, mine(1 - c)].astype(BF16)
    swap = remote(half_out, half_in, half_send, half_got, pair)
    swap.start()
    swap.wait_recv()
    pieces[...] = (partial[:, mine(c)] + half_in[...].astype(F32)).astype(BF16).reshape(RING, PART, 256)

    def piece_to(p):
        return remote(pieces.at[p], pieces_all.at[me], piece_send, piece_got, chip(p))

    across(lambda p: piece_to(p).start())
    pieces_all[me] = pieces[me]
    all_but_one(pieces_all, piece_got)
    total[...] = sum(pieces_all[k].astype(F32) for k in range(RING)).astype(BF16)

    def pass_on(p):
        return remote(totals.at[c, p], totals.at[c, p], last_send, last_got, pair)

    for n, (a, b) in enumerate(PLANE):
        p = 4 * lax.rem(x + a, 4) + lax.rem(y + b, 4)
        remote(total, totals.at[c, me], total_send, total_got.at[n // 5], chip(p)).start()
    totals[c, me] = total[...]
    pass_on(me).start()
    for g in range(3):
        five = pieces.at[pl.ds(0, 5)]
        pltpu.make_async_copy(five, five, total_got.at[g]).wait()
        for a, b in PLANE[5 * g : 5 * g + 5]:
            pass_on(4 * lax.rem(x + 4 - a, 4) + lax.rem(y + 4 - b, 4)).start()
    pltpu.make_async_copy(totals.at[1 - c], totals.at[1 - c], last_got).wait()
    grad_out[:, 0:256] = totals[0].reshape(D, 256)
    grad_out[:, 256:SHARD] = totals[1].reshape(D, 256)[:, : SHARD - 256]

    pltpu.make_async_copy(totals.at[c], totals.at[c], last_send).wait()
    swap.wait_send()
    all_but_one(names_all, name_send)
    all_but_one(stats, stat_send)
    all_but_one(notes_all, note_send)
    all_but_one(pieces, piece_send)
    all_but_one(pieces, total_send)

    def ring_sent(i):
        for h in range(2):
            rise(i, h).wait_send()

            @pl.when(i < 7)
            def _():
                sink(i, h).wait_send()

    loop(0, 8, ring_sent)


MOE_SCRATCH = [
    VMEM((LAYERS, D, EFF), BF16),
    VMEM((LAYERS, EFF, D), BF16),
    VMEM((8, D), F32),
    VMEM((LAYERS, 16, D), BF16),
    VMEM((LAYERS, 8, D), F32),
    VMEM((TOK, D), BF16),
    VMEM((RING, 16, HALF), BF16),
    VMEM((RING, 16, HALF), BF16),
    VMEM((RING, 16, HALF), BF16),
    VMEM((RING, 16, HALF), BF16),
    VMEM((TURNS, IN_ROWS, EFF), BF16),
    VMEM((TURNS, OUT_ROWS, D), BF16),
    VMEM((2, FRAMES, HALF), BF16),
    VMEM((2, FRAMES, HALF), BF16),
    DMA((CHUNKS,)), DMA((CHUNKS,)), DMA, DMA,
    DMA((LAYERS,)), DMA((LAYERS,)), DMA((LAYERS,)), DMA((LAYERS,)),
    DMA((4, TURNS)), DMA((2, TURNS)), DMA((2, TURNS)), DMA((2, 4)), DMA((2, LAYERS)),
    DMA, DMA, DMA, DMA,
    DMA, DMA, DMA,
]
HEAD_SCRATCH = [
    VMEM((RING, 2, FRAMES, HALF), BF16),
    VMEM((8, 128), F32),
    VMEM((RING, 8, 128), F32),
    VMEM((RING * FRAMES, WIDE), F32),
    VMEM((RING, 8, 128), F32),
    VMEM((RING, 8, 128), F32),
    VMEM((FRAMES, 128), F32),
    VMEM((FRAMES, 128), F32),
    VMEM((FRAMES, 128), F32),
    VMEM((8, 128), F32),
    VMEM((RING, 8, 128), F32),
    VMEM((RING * FRAMES, WIDE), BF16),
    VMEM((D, WIDE), F32),
    VMEM((D, 256), BF16),
    VMEM((D, 256), BF16),
    VMEM((RING, PART, 256), BF16),
    VMEM((RING, PART, 256), BF16),
    VMEM((PART, 256), BF16),
    VMEM((2, RING, PART, 256), BF16),
    DMA((8, 2)), DMA((8, 2)), DMA((8, 2)), DMA((8, 2)),
    DMA, DMA, DMA, DMA, DMA, DMA,
    DMA, DMA,
    DMA, DMA, DMA, DMA((3,)),
    DMA, DMA,
]


def whole_kernel(
    frames, w_in, w_out, router, gain, routes, head_gain, head_weight, numbers, loss_out, grad_out,
    hn, weight, weight_got, *scratch,
):
    fetch = pltpu.make_async_copy(head_weight, weight, weight_got)
    fetch.start()
    moe_kernel(frames, w_in, w_out, router, gain, routes, head_gain, hn, *scratch[: len(MOE_SCRATCH)])
    head_kernel(fetch, hn, weight, numbers, loss_out, grad_out, *scratch[len(MOE_SCRATCH) :])


def run(*arrays):
    anywhere, local = pl.BlockSpec(memory_space=pl.ANY), pl.BlockSpec(memory_space=VMEM)
    return pl.pallas_call(
        whole_kernel,
        out_shape=(jax.ShapeDtypeStruct((8, 128), F32), jax.ShapeDtypeStruct((D, SHARD), BF16)),
        in_specs=[anywhere] * 3 + [local] * 4 + [anywhere, local],
        out_specs=(local, local),
        scratch_shapes=[VMEM((2, FRAMES, HALF), BF16), VMEM((D, SHARD), BF16), DMA] + MOE_SCRATCH + HEAD_SCRATCH,
        compiler_params=pltpu.CompilerParams(
            collective_id=0, has_side_effects=True, vmem_limit_bytes=VMEM_LIMIT
        ),
    )(*arrays)


def per_device(
    frames,
    norm_gain,
    router,
    w_in,
    w_out,
    routing,
    head_gain,
    head_weight,
    frame_lengths,
    labels,
    label_lengths,
):
    micro = frames.shape[0]
    routes = routing[0, :, :, :, 0].reshape(micro, TOK).astype(F32)
    routes = jnp.pad(routes, ((0, 8 - micro), (0, 128 - TOK)), constant_values=-1.0)
    pairs, count = 2 * micro, labels.shape[2]
    numbers = jnp.concatenate(
        [labels.reshape(pairs, count), frame_lengths.reshape(pairs, 1), label_lengths.reshape(pairs, 1)], axis=1
    )
    numbers = jnp.pad(numbers.astype(F32), ((0, 0), (0, 128 - numbers.shape[1])))
    losses, grad = run(
        frames.reshape(micro, TOK, D), w_in[0, 0], w_out[0, 0], router[0].T, norm_gain, routes,
        head_gain.reshape(1, D), head_weight, numbers,
    )
    return losses[0:1, 0:1], grad


def solution(mesh):
    placed = (
        P(None, ("expert", "dp"), None, None),
        P("section", None),
        P("section", None, None),
        P("section", "expert", None, None),
        P("section", "expert", None, None),
        P("section", None, ("expert", "dp"), None, None),
        P(),
        P(None, "expert"),
        P(None, ("expert", "dp")),
        P(None, ("expert", "dp"), None),
        P(None, ("expert", "dp")),
    )
    return jax.shard_map(
        per_device,
        mesh=mesh,
        in_specs=placed,
        out_specs=(P("section", ("expert", "dp")), P(None, "expert")),
        check_vma=False,
    )
```

```python
import functools

import jax
import jax.numpy as jnp
from jax import lax
from jax.experimental import pallas as pl
from jax.experimental.pallas import tpu as pltpu
from jax.sharding import PartitionSpec as P

EPSILON = 1e-06
LOG_ZERO = -1e30
MESH = pl.DeviceIdType.MESH
F32, BF16 = jnp.float32, jnp.bfloat16
D, HALF, EFF, LAYERS, RING, TOK, FRAMES = 1280, 640, 256, 8, 16, 96, 48
PIECES = 16
SKEW = 4
TURNS = PIECES // 4
CHUNKS = LAYERS * PIECES
IN_ROWS, OUT_ROWS = D // PIECES, EFF // PIECES
SHARD, WIDE = 500, 512
PART = WIDE // 2 // RING
HIGHEST = lax.Precision.HIGHEST
VMEM = pltpu.VMEM
DMA = pltpu.SemaphoreType.DMA
VMEM_LIMIT = 56 * 1024 * 1024
PLANE = sorted([(a, b) for a in range(4) for b in range(4) if a or b], key=lambda d: -sum(min(v, 4 - v) for v in d))
AROUND = sorted(range(1, RING), key=lambda d: -min(d, RING - d))


def coords():
    s, z, y = lax.axis_index("section"), lax.axis_index("expert"), lax.axis_index("dp")
    return s, s // 2, lax.rem(s, 2), z, y


def loop(low, high, body):
    def step(i, carry):
        body(i)
        return carry

    lax.fori_loop(low, high, step, 0)


def remote(src, dst, send, recv, device):
    return pltpu.make_async_remote_copy(
        src_ref=src, dst_ref=dst, send_sem=send, recv_sem=recv, device_id=device, device_id_type=MESH
    )


def dot(a, b, dims=((1,), (0,)), precision=None):
    return lax.dot_general(a, b, (dims, ((), ())), precision=precision, preferred_element_type=F32)


def rms(x, gain):
    return (x * lax.rsqrt(jnp.mean(x * x, axis=-1, keepdims=True) + EPSILON) * gain).astype(BF16)


def moe_kernel(
    frames, w_in, w_out, router, gain, routes, head_gain, hn_out,
    win, wout, aux, routers, auxes, state, give, take, answer, back, stage_in, stage_out, passed, landed,
    got_in, got_out, on_in, on_out, copy_in, copy_out, have_in, have_out,
    lay_send, stage_send, stage_got, small_send, small_got, give_send, take_got, answer_send, back_got, hn_send, hn_got, state_got,
):
    s, x, c, z, y = coords()
    me = 4 * x + y
    home_x, home_y = z // 4, lax.rem(z, 4)
    above, below = lax.rem(z + 1, RING), lax.rem(z + RING - 1, RING)
    barrier = pltpu.get_barrier_semaphore()

    def greet(i):
        p = lax.rem(4 * s + y + i, 32)
        pl.semaphore_signal(barrier, inc=1, device_id=(p // 4, z, lax.rem(p, 4)), device_id_type=MESH)

    for i in range(1, 32):
        greet(i)

    def greet_ring(i):
        pl.semaphore_signal(barrier, inc=1, device_id=(s, lax.rem(z + i, RING), y), device_id_type=MESH)

    for i in range(1, RING):
        greet_ring(i)
    pl.semaphore_wait(barrier, 46)

    def in_rows(j):
        return pl.ds(pl.multiple_of(j * IN_ROWS, 16), IN_ROWS)

    def out_rows(j):
        return pl.ds(pl.multiple_of(j * OUT_ROWS, 16), OUT_ROWS)

    def share(layer, i, src_in, src_out):
        j = y + 4 * i
        k = layer * PIECES + j
        target = (2 * home_x + 1, z, home_y)
        return (
            remote(src_in, win.at[layer, in_rows(j)], lay_send.at[2 * c, i], got_in.at[k], target),
            remote(src_out, wout.at[layer, out_rows(j)], lay_send.at[2 * c + 1, i], got_out.at[k], target),
        )

    def staged(i):
        j = y + 4 * i
        target = (s + 1, z, y)
        return (
            remote(w_in.at[in_rows(j)], stage_in.at[i], stage_send.at[0, i], stage_got.at[0, i], target),
            remote(w_out.at[out_rows(j)], stage_out.at[i], stage_send.at[1, i], stage_got.at[1, i], target),
        )

    def small(to_x):
        target = (2 * to_x, z, y)
        return (
            remote(aux, auxes.at[s], small_send.at[0, to_x], small_got.at[0, s], target),
            remote(router, routers.at[s], small_send.at[1, to_x], small_got.at[1, s], target),
        )

    def each(copies, act):
        for copy in copies:
            act(copy)

    start, sent, got = (lambda d: d.start()), (lambda d: d.wait_send()), (lambda d: d.wait_recv())

    @pl.when((c == 0) & (x == 0))
    def _():
        for i in range(TURNS):
            each(share(0, i, w_in.at[in_rows(y + 4 * i)], w_out.at[out_rows(y + 4 * i)]), start)

    @pl.when((c == 0) & (x > 0))
    def _():
        for i in range(TURNS):
            each(staged(i), start)

    rows, cols = lax.broadcasted_iota(jnp.int32, (128, 128), 0), lax.broadcasted_iota(jnp.int32, (128, 128), 1)
    aux[...] = jnp.zeros_like(aux)
    aux[0:1, :] = gain[...]
    for m in range(4):
        named = jnp.broadcast_to(routes[m : m + 1, :], (128, 128))
        before = (jnp.transpose(named) == named) & (rows < cols)
        rank = jnp.sum(before.astype(F32), axis=0, keepdims=True)
        live = lax.broadcasted_iota(jnp.int32, (1, 128), 1) < TOK
        aux[m + 1 : m + 2, 0:128] = jnp.where(live, 8.0 * routes[m : m + 1, :] + rank, -1.0)

    for gap in range(1, 4):
        each(small(lax.rem(x + gap, 4)), start)

    own_small = (
        pltpu.make_async_copy(aux, auxes.at[s], small_got.at[0, s]),
        pltpu.make_async_copy(router, routers.at[s], small_got.at[1, s]),
    )

    @pl.when(c == 1)
    def _():
        each(small(x), start)

    @pl.when(c == 0)
    def _():
        each(own_small, start)

    @pl.when(c == 1)
    def _():
        at_home = (x == home_x) & (y == home_y)
        up, down = lax.rem(z + RING - me, RING), lax.rem(me + RING - z, RING)

        def distribute(layer, slot, pick):
            for i in range(TURNS):
                j = y + 4 * i
                src_in, src_out = pick(i)

                @pl.when(at_home)
                def _():
                    k = layer * PIECES + j
                    pltpu.make_async_copy(src_in, win.at[layer, in_rows(j)], got_in.at[k]).start()
                    pltpu.make_async_copy(src_out, wout.at[layer, out_rows(j)], got_out.at[k]).start()

                @pl.when(jnp.logical_not(at_home))
                def _():
                    each(carried(layer, slot, i, src_in, src_out), start)

        def carried(layer, slot, i, src_in, src_out):
            j = y + 4 * i
            k = layer * PIECES + j
            target = (2 * home_x + 1, z, home_y)
            return (
                remote(src_in, win.at[layer, in_rows(j)], lay_send.at[2 * slot, i], got_in.at[k], target),
                remote(src_out, wout.at[layer, out_rows(j)], lay_send.at[2 * slot + 1, i], got_out.at[k], target),
            )

        def from_stage(i):
            return stage_in.at[i], stage_out.at[i]

        def from_own(i):
            return w_in.at[in_rows(y + 4 * i)], w_out.at[out_rows(y + 4 * i)]

        def rise(k):
            layer, j = k // PIECES, lax.rem(k, PIECES)
            ref = win.at[layer, in_rows(j)]
            return remote(ref, ref, on_in, got_in.at[k], (s, above, y))

        def sink(k):
            layer, j = k // PIECES, lax.rem(k, PIECES)
            ref = wout.at[layer, out_rows(j)]
            return remote(ref, ref, on_out, got_out.at[k], (s, below, y))

        def hand_in(layer):
            return remote(win.at[layer], win.at[layer], copy_in.at[layer], have_in.at[layer], (s - 1, z, y))

        def hand_out(layer):
            return remote(wout.at[layer], wout.at[layer], copy_out.at[layer], have_out.at[layer], (s - 1, z, y))

        def tick(t):
            @pl.when((x > 0) & (t == PIECES * (2 * x - 1)))
            def _():
                for i in range(TURNS):
                    each(staged(i), got)
                distribute(2 * x, 0, from_stage)

            @pl.when(t == 2 * PIECES * x)
            def _():
                distribute(2 * x + 1, 1, from_own)

            ku, kd = t - SKEW * up, t - SKEW * down

            @pl.when((ku >= 0) & (ku < CHUNKS))
            def _():
                rise(ku).wait_recv()

                @pl.when(up < RING - 1)
                def _():
                    rise(ku).start()

                @pl.when(lax.rem(ku, PIECES) == PIECES - 1)
                def _():
                    hand_in(ku // PIECES).start()

            @pl.when((kd >= 0) & (kd < CHUNKS))
            def _():
                sink(kd).wait_recv()

                @pl.when(down < RING - 1)
                def _():
                    sink(kd).start()

                @pl.when(lax.rem(kd, PIECES) == PIECES - 1)
                def _():
                    hand_out(kd // PIECES).start()

        loop(0, CHUNKS + SKEW * (RING - 1), tick)

        @pl.when(jnp.logical_not(at_home))
        def _():
            for i in range(TURNS):
                @pl.when(x > 0)
                def _():
                    each(carried(2 * x, 0, i, *from_stage(i)), sent)

                each(carried(2 * x + 1, 1, i, *from_own(i)), sent)

        @pl.when(up < RING - 1)
        def _():
            pltpu.make_async_copy(win, win, on_in).wait()

        @pl.when(down < RING - 1)
        def _():
            pltpu.make_async_copy(wout, wout, on_out).wait()

        loop(0, LAYERS, lambda layer: hand_in(layer).wait_send())
        loop(0, LAYERS, lambda layer: hand_out(layer).wait_send())
        each(small(x), sent)

    @pl.when(c == 0)
    def _():
        pltpu.make_async_copy(frames.at[x], state, state_got).start()

        def smalls(layer):
            pltpu.make_async_copy(aux, auxes.at[layer], small_got.at[0, layer]).wait()
            pltpu.make_async_copy(router, routers.at[layer], small_got.at[1, layer]).wait()

        loop(0, LAYERS, smalls)
        pltpu.make_async_copy(frames.at[x], state, state_got).wait()

        def chip(p):
            return (2 * (p // 4), z, lax.rem(p, 4))

        def out_to(p):
            return remote(give.at[p], take.at[me], give_send, take_got, chip(p))

        def back_to(p):
            return remote(answer.at[p], back.at[me], answer_send, back_got, chip(p))

        def start_all(copy):
            for i in range(1, RING):
                copy(lax.rem(me + i, RING)).start()

        def wait_all(buffer, sem):
            most = buffer.at[pl.ds(0, RING - 1)]
            pltpu.make_async_copy(most, most, sem).wait()

        def layer_step(layer):
            xf = state[...].astype(F32)
            normed = rms(xf, auxes[layer, 0:1, :])
            which = lax.broadcasted_iota(jnp.int32, (8, 128), 0) == 1 + x
            spots = jnp.sum(jnp.where(which, auxes[layer, :, 0:128], 0.0), axis=0, keepdims=True)
            pick = (lax.broadcasted_iota(jnp.int32, (128, 128), 0).astype(F32) == spots)[:, :TOK]
            pick = pick.astype(F32).astype(BF16)
            left = dot(pick, normed[:, :HALF]).reshape(RING, 8, HALF)
            right = dot(pick, normed[:, HALF:]).reshape(RING, 8, HALF)
            give[...] = jnp.concatenate([left, right], axis=1).astype(BF16)
            start_all(out_to)
            take[me] = give[me]

            columns = jnp.transpose(jnp.broadcast_to(spots, (128, 128)))[:TOK, :].astype(jnp.int32)
            lane = lax.broadcasted_iota(jnp.int32, (TOK, 128), 1)
            logits = dot(normed, routers[layer], ((1,), (1,)))
            mine = (lane[:, :RING] == (columns[:, :RING] >> 3)).astype(F32)
            gate = jax.nn.sigmoid(jnp.sum(mine * logits, axis=1, keepdims=True))
            place = columns + ((columns >> 3) << 3)
            spread = [(lane + 128 * h == place + 8 * b).astype(F32).astype(BF16) for b in range(2) for h in range(2)]
            put_left = jnp.concatenate(spread[:2], axis=1)
            put_right = jnp.concatenate(spread[2:], axis=1)

            pltpu.make_async_copy(win.at[layer], win.at[layer], have_in.at[layer]).wait()
            wait_all(take, take_got)
            rows = take[...].reshape(RING * 16, HALF)
            first = dot(rows, win[layer, 0:HALF, :]).reshape(RING, 16, EFF)
            second = dot(rows, win[layer, HALF:D, :]).reshape(RING, 16, EFF)
            hidden = (first[:, 0:8] + second[:, 8:16]).reshape(128, EFF)
            active = (hidden * jax.nn.sigmoid(hidden)).astype(BF16)
            pltpu.make_async_copy(wout.at[layer], wout.at[layer], have_out.at[layer]).wait()
            result = dot(active, wout[layer]).reshape(RING, 8, D)
            answer[...] = jnp.concatenate([result[:, :, :HALF], result[:, :, HALF:]], axis=1).astype(BF16)
            start_all(back_to)
            back[me] = answer[me]
            wait_all(give, give_send)
            wait_all(back, back_got)
            returned = back[...].reshape(RING * 16, HALF)
            mixed = jnp.concatenate([dot(put_left, returned), dot(put_right, returned)], axis=1)
            state[...] = (xf + gate * mixed).astype(BF16)
            wait_all(answer, answer_send)

        loop(0, LAYERS, layer_step)
        hn = rms(state[...].astype(F32), head_gain[...])
        for h in range(2):
            hn_out[h] = hn[:FRAMES, HALF * h : HALF * (h + 1)]
            passed[h] = hn[FRAMES:, HALF * h : HALF * (h + 1)]
        remote(passed, landed, hn_send, hn_got, (s + 1, z, y)).start()

        @pl.when(x == 0)
        def _():
            for i in range(TURNS):
                each(share(0, i, w_in.at[in_rows(y + 4 * i)], w_out.at[out_rows(y + 4 * i)]), sent)

        @pl.when(x > 0)
        def _():
            for i in range(TURNS):
                each(staged(i), sent)

        remote(passed, landed, hn_send, hn_got, (s + 1, z, y)).wait_send()

    @pl.when(c == 1)
    def _():
        remote(passed, landed, hn_send, hn_got, (s, z, y)).wait_recv()
        hn_out[...] = landed[...]

    for gap in range(1, 4):
        each(small(lax.rem(x + gap, 4)), sent)


def flip(block):
    rows = block.shape[0]
    if rows < 128:
        block = jnp.concatenate([block, jnp.zeros((128 - rows, 128), F32)], axis=0)
    return jnp.transpose(block)


def pack(columns):
    turned = flip(columns)
    return turned[0:8] + pltpu.roll(turned[8:16], 64, 1)


def lanes(rows):
    return lax.broadcasted_iota(jnp.int32, (rows, 128), 1)


def triple(a, b, c):
    top = jnp.maximum(jnp.maximum(a, b), c)
    return top + jnp.log(jnp.exp(a - top) + jnp.exp(b - top) + jnp.exp(c - top))


def head_kernel(
    fetch, hn, weight, numbers, loss_out, grad_out,
    rows_all, names, names_all, chosen_all, logits, stats, stats_all, emit, ahead, behind, notes, notes_all, grads, partial,
    half_out, half_in, pieces, pieces_all, total, totals,
    up_send, up_got, down_send, down_got, name_send, name_got, stat_send, stat_got, note_send, note_got,
    half_send, half_got, piece_send, piece_got, total_send, total_got, last_send, last_got,
):
    s, x, c, z, y = coords()
    me = 4 * x + y
    pair = (s + 1 - 2 * c, z, y)
    above, below = lax.rem(z + 1, RING), lax.rem(z + RING - 1, RING)

    def chip(p):
        return (2 * (p // 4) + c, z, lax.rem(p, 4))

    def along(act):
        for i in AROUND:
            act(lax.rem(z + i, RING))

    def across(act):
        for a, b in PLANE:
            act(4 * lax.rem(x + a, 4) + lax.rem(y + b, 4))

    def rise(i, h):
        block = rows_all.at[lax.rem(z + RING - i, RING), h]
        return remote(block, block, up_send.at[i, h], up_got.at[i, h], (s, above, y))

    def sink(i, h):
        block = rows_all.at[lax.rem(z + i, RING), h]
        return remote(block, block, down_send.at[i, h], down_got.at[i, h], (s, below, y))

    def risen(i, h):
        block = rows_all.at[lax.rem(z + RING - i, RING), h]
        return remote(block, block, up_send.at[i - 1, h], up_got.at[i - 1, h], (s, above, y))

    def sunk(i, h):
        block = rows_all.at[lax.rem(z + i, RING), h]
        return remote(block, block, down_send.at[i - 1, h], down_got.at[i - 1, h], (s, below, y))

    rows_all[z] = hn[...]
    for h in range(2):
        rise(0, h).start()
        sink(0, h).start()

    one = lanes(1)
    chosen = lax.broadcasted_iota(jnp.int32, (8, 128), 0) == s
    known_row = jnp.sum(jnp.where(chosen, numbers[...], 0.0), axis=0, keepdims=True)
    tags = jnp.where(one < 12, known_row, jnp.where(one == 12, 0.0, -2.0))
    names[...] = jnp.broadcast_to(tags, (8, 128))

    def all_but_one(buffer, sem):
        most = buffer.at[pl.ds(0, RING - 1)]
        pltpu.make_async_copy(most, most, sem).wait()

    def name_to(p):
        return remote(names, names_all.at[z], name_send, name_got, (s, p, y))

    along(lambda p: name_to(p).start())
    fetch.wait()
    names_all[z] = names[...]
    logits[:, WIDE - 128 : WIDE] = jnp.zeros((RING * FRAMES, 128), F32)

    columns = lax.broadcasted_iota(jnp.int32, (128, WIDE), 1)
    valid = columns[:FRAMES] < SHARD
    owned = jnp.where(columns < SHARD, columns + SHARD * z, -1).astype(F32)

    def selector(k):
        wanted = flip(jnp.broadcast_to(names_all[k, 0:1, :], (128, 128)))
        return (jnp.concatenate([wanted] * 4, axis=1) == owned).astype(F32).astype(BF16)

    def thirds(value):
        high = value.astype(BF16)
        rest = value - high.astype(F32)
        middle = rest.astype(BF16)
        return jnp.concatenate([high, middle, (rest - middle.astype(F32)).astype(BF16)], axis=0)

    def joined(parts):
        return parts[0:FRAMES] + parts[FRAMES : 2 * FRAMES] + parts[2 * FRAMES :]

    def frames_of(k):
        return pl.ds(pl.multiple_of(k * FRAMES, FRAMES), FRAMES)

    lane = lanes(FRAMES)

    def stat_to(p):
        return remote(stats.at[p], stats_all.at[z], stat_send, stat_got, (s, p, y))

    def evaluate(blocks):
        def side(h):
            return jnp.concatenate([rows_all[k, h] for k in blocks], axis=0)

        value = dot(side(0), weight[:, 0:HALF], ((1,), (1,))) + dot(side(1), weight[:, HALF:D], ((1,), (1,)))
        for n, k in enumerate(blocks):
            logits[frames_of(k), 0:SHARD] = value[n * FRAMES : (n + 1) * FRAMES]
        for k in blocks:
            block = logits[frames_of(k), :]
            peak = jnp.max(jnp.where(valid, block, -jnp.inf), axis=1, keepdims=True)
            weightsum = jnp.sum(jnp.where(valid, jnp.exp(block - peak), 0.0), axis=1, keepdims=True)
            chosen_all[k] = selector(k)
            found = joined(dot(thirds(block), chosen_all[k], ((1,), (1,))))
            stats[k] = pack(jnp.where(lane == 13, peak, jnp.where(lane == 14, weightsum, found)))

    def ring_step(i):
        for h in range(2):
            risen(i, h).wait_recv()

            @pl.when(i < 8)
            def _():
                rise(i, h).start()
                sunk(i, h).wait_recv()

            @pl.when(i < 7)
            def _():
                sink(i, h).start()

        @pl.when(i == 1)
        def _():
            all_but_one(names_all, name_got)

        lower, upper = lax.rem(z + RING + 1 - i, RING), lax.rem(z + i - 1, RING)
        evaluate((lower, upper))

        @pl.when(i > 1)
        def _():
            stat_to(lower).start()
            stat_to(upper).start()

    loop(1, 9, ring_step)
    opposite = lax.rem(z + 8, RING)
    evaluate((opposite,))
    stat_to(opposite).start()
    stats_all[z] = stats[z]
    all_but_one(stats_all, stat_got)

    low = [stats_all[k] for k in range(RING)]
    high = [pltpu.roll(v, 64, 1) for v in low]
    peaks = functools.reduce(jnp.maximum, high)
    sums = sum(v * pltpu.roll(jnp.exp(v - peaks), 1, 0) for v in high)
    live = lanes(1) < FRAMES
    log_total = jnp.where(live, peaks[5:6] + jnp.log(jnp.where(live, sums[6:7], 1.0)), 0.0)
    both = jnp.concatenate([sum(low), sum(high)], axis=0)
    slot = lax.broadcasted_iota(jnp.int32, (16, 128), 0)
    both = jnp.where(lanes(16) < FRAMES, both - log_total, 0.0)
    both = jnp.where(slot < 13, both, jnp.where(slot == 14, log_total, 0.0))
    by_label = flip(both)
    row, col = lax.broadcasted_iota(jnp.int32, (128, 128), 0), lanes(128)
    odd = (col & 1) == 1
    expand = (col < 25) & (jnp.where(odd, col >> 1, 12) == row)
    expand = expand.astype(F32)
    emit[...] = dot(by_label[:FRAMES], expand, precision=HIGHEST)
    total_col = by_label[:FRAMES]
    span = jnp.sum(jnp.where(one == 12, known_row, 0.0), axis=1, keepdims=True)
    last = 2.0 * jnp.sum(jnp.where(one == 13, known_row, 0.0), axis=1, keepdims=True)
    differs = (known_row != pltpu.roll(known_row, 1, 1)) & (known_row != 0.0) & (one > 0) & (one < 12)
    jumps = dot(jnp.broadcast_to(differs.astype(F32), (8, 128)), expand)[0:1]
    jump, jump_back = jumps > 0.5, pltpu.roll(jumps, 126, 1) > 0.5
    spot = one.astype(F32)
    ends = (spot == last) | (spot == last - 1.0)
    closing = jnp.where(ends, 0.0, LOG_ZERO)
    opening = jnp.where(one < 2, emit[0:1, :], LOG_ZERO)
    ahead[0:1, :] = opening
    behind[FRAMES - 1 : FRAMES, :] = closing

    def ctc_step(i, carry):
        a, b = carry
        once = jnp.where(one < 1, LOG_ZERO, pltpu.roll(a, 1, 1))
        twice = jnp.where(jump, pltpu.roll(a, 2, 1), LOG_ZERO)
        moved = triple(a, once, twice) + emit[pl.ds(i, 1), :]
        a = jnp.where(i.astype(F32) < span, moved, a)
        ahead[pl.ds(i, 1), :] = a
        t = FRAMES - 1 - i
        g = b + emit[pl.ds(t + 1, 1), :]
        once = jnp.where(one > 126, LOG_ZERO, pltpu.roll(g, 127, 1))
        twice = jnp.where(jump_back, pltpu.roll(g, 126, 1), LOG_ZERO)
        b = jnp.where(t.astype(F32) < span - 1.0, triple(g, once, twice), closing)
        behind[pl.ds(t, 1), :] = b
        return a, b

    final, _ = lax.fori_loop(1, FRAMES, ctc_step, (opening, closing))
    tail = jnp.where(ends, final, LOG_ZERO)
    top = jnp.max(tail, axis=1, keepdims=True)
    likely = top + jnp.log(jnp.sum(jnp.where(ends, jnp.exp(final - top), 0.0), axis=1, keepdims=True))
    loss_out[...] = jnp.broadcast_to(-likely, (8, 128))
    when = lax.broadcasted_iota(jnp.int32, (FRAMES, 128), 0).astype(F32)
    occupied = jnp.where(
        (when < span) & (lane < 25), -jnp.exp(ahead[...] + behind[...] - likely), 0.0
    )
    merged = dot(occupied, expand, ((1,), (1,)), HIGHEST)
    mass = jnp.sum(occupied, axis=1, keepdims=True)
    notes[...] = pack(
        jnp.where(lane == 13, mass, jnp.where(lane == 14, total_col, jnp.where(lane < 13, merged, 0.0)))
    )
    notes_all[z] = notes[...]

    def note_to(p):
        return remote(notes, notes_all.at[z], note_send, note_got, (s, p, y))

    along(lambda p: note_to(p).start())
    all_but_one(notes_all, note_got)

    def spread(group):
        for k in [4 * group + n for n in range(4)]:
            packed = notes_all[k]
            known = flip(jnp.concatenate([packed, pltpu.roll(packed, 64, 1)], axis=0))[:FRAMES]
            scattered = joined(dot(thirds(known), chosen_all[k]))
            block = logits[frames_of(k), :]
            value = scattered - jnp.exp(block - known[:, 14:15]) * known[:, 13:14]
            grads[frames_of(k), :] = jnp.where(valid, value, 0.0).astype(BF16)

    loop(0, RING // 4, spread)
    for h in range(2):
        partial[:, HALF * h : HALF * (h + 1)] = dot(
            grads[...], rows_all[:, h].reshape(RING * FRAMES, HALF), ((0,), (0,))
        )

    def mine(core):
        return pl.ds(pl.multiple_of(256 * core, 256), 256)

    half_out[...] = partial[mine(1 - c), :].astype(BF16)
    swap = remote(half_out, half_in, half_send, half_got, pair)
    swap.start()
    swap.wait_recv()
    pieces[...] = (partial[mine(c), :] + half_in[...].astype(F32)).astype(BF16).reshape(RING, PART, D)

    def piece_to(p):
        return remote(pieces.at[p], pieces_all.at[me], piece_send, piece_got, chip(p))

    across(lambda p: piece_to(p).start())
    pieces_all[me] = pieces[me]
    all_but_one(pieces_all, piece_got)
    total[...] = sum(pieces_all[k].astype(F32) for k in range(RING)).astype(BF16)

    def pass_on(p):
        return remote(totals.at[c, p], totals.at[c, p], last_send, last_got, pair)

    for n, (a, b) in enumerate(PLANE):
        p = 4 * lax.rem(x + a, 4) + lax.rem(y + b, 4)
        remote(total, totals.at[c, me], total_send, total_got.at[n // 5], chip(p)).start()
    totals[c, me] = total[...]
    pass_on(me).start()
    for g in range(3):
        five = pieces.at[pl.ds(0, 5)]
        pltpu.make_async_copy(five, five, total_got.at[g]).wait()
        for a, b in PLANE[5 * g : 5 * g + 5]:
            pass_on(4 * lax.rem(x + 4 - a, 4) + lax.rem(y + 4 - b, 4)).start()
    pltpu.make_async_copy(totals.at[1 - c], totals.at[1 - c], last_got).wait()
    grad_out[0:256, :] = totals[0].reshape(256, D)
    grad_out[256:SHARD, :] = totals[1].reshape(256, D)[: SHARD - 256, :]

    pltpu.make_async_copy(totals.at[c], totals.at[c], last_send).wait()
    swap.wait_send()
    all_but_one(names_all, name_send)
    all_but_one(stats, stat_send)
    all_but_one(notes_all, note_send)
    all_but_one(pieces, piece_send)
    all_but_one(pieces, total_send)

    def ring_sent(i):
        for h in range(2):
            rise(i, h).wait_send()

            @pl.when(i < 7)
            def _():
                sink(i, h).wait_send()

    loop(0, 8, ring_sent)


MOE_SCRATCH = [
    VMEM((LAYERS, D, EFF), BF16),
    VMEM((LAYERS, EFF, D), BF16),
    VMEM((8, D), F32),
    VMEM((LAYERS, 16, D), BF16),
    VMEM((LAYERS, 8, D), F32),
    VMEM((TOK, D), BF16),
    VMEM((RING, 16, HALF), BF16),
    VMEM((RING, 16, HALF), BF16),
    VMEM((RING, 16, HALF), BF16),
    VMEM((RING, 16, HALF), BF16),
    VMEM((TURNS, IN_ROWS, EFF), BF16),
    VMEM((TURNS, OUT_ROWS, D), BF16),
    VMEM((2, FRAMES, HALF), BF16),
    VMEM((2, FRAMES, HALF), BF16),
    DMA((CHUNKS,)), DMA((CHUNKS,)), DMA, DMA,
    DMA((LAYERS,)), DMA((LAYERS,)), DMA((LAYERS,)), DMA((LAYERS,)),
    DMA((4, TURNS)), DMA((2, TURNS)), DMA((2, TURNS)), DMA((2, 4)), DMA((2, LAYERS)),
    DMA, DMA, DMA, DMA,
    DMA, DMA, DMA,
]
HEAD_SCRATCH = [
    VMEM((RING, 2, FRAMES, HALF), BF16),
    VMEM((8, 128), F32),
    VMEM((RING, 8, 128), F32),
    VMEM((RING, 128, WIDE), BF16),
    VMEM((RING * FRAMES, WIDE), F32),
    VMEM((RING, 8, 128), F32),
    VMEM((RING, 8, 128), F32),
    VMEM((FRAMES, 128), F32),
    VMEM((FRAMES, 128), F32),
    VMEM((FRAMES, 128), F32),
    VMEM((8, 128), F32),
    VMEM((RING, 8, 128), F32),
    VMEM((RING * FRAMES, WIDE), BF16),
    VMEM((WIDE, D), F32),
    VMEM((256, D), BF16),
    VMEM((256, D), BF16),
    VMEM((RING, PART, D), BF16),
    VMEM((RING, PART, D), BF16),
    VMEM((PART, D), BF16),
    VMEM((2, RING, PART, D), BF16),
    DMA((8, 2)), DMA((8, 2)), DMA((8, 2)), DMA((8, 2)),
    DMA, DMA, DMA, DMA, DMA, DMA,
    DMA, DMA,
    DMA, DMA, DMA, DMA((3,)),
    DMA, DMA,
]


def whole_kernel(
    frames, w_in, w_out, router, gain, routes, head_gain, head_weight, numbers, loss_out, grad_out,
    hn, weight, weight_got, *scratch,
):
    fetch = pltpu.make_async_copy(head_weight, weight, weight_got)
    fetch.start()
    moe_kernel(frames, w_in, w_out, router, gain, routes, head_gain, hn, *scratch[: len(MOE_SCRATCH)])
    head_kernel(fetch, hn, weight, numbers, loss_out, grad_out, *scratch[len(MOE_SCRATCH) :])


def run(*arrays):
    anywhere, local = pl.BlockSpec(memory_space=pl.ANY), pl.BlockSpec(memory_space=VMEM)
    return pl.pallas_call(
        whole_kernel,
        out_shape=(jax.ShapeDtypeStruct((8, 128), F32), jax.ShapeDtypeStruct((SHARD, D), BF16)),
        in_specs=[anywhere] * 3 + [local] * 4 + [anywhere, local],
        out_specs=(local, local),
        scratch_shapes=[VMEM((2, FRAMES, HALF), BF16), VMEM((SHARD, D), BF16), DMA] + MOE_SCRATCH + HEAD_SCRATCH,
        compiler_params=pltpu.CompilerParams(
            collective_id=0, has_side_effects=True, vmem_limit_bytes=VMEM_LIMIT
        ),
    )(*arrays)


def per_device(
    frames,
    norm_gain,
    router,
    w_in,
    w_out,
    routing,
    head_gain,
    head_weight,
    frame_lengths,
    labels,
    label_lengths,
):
    micro = frames.shape[0]
    routes = routing[0, :, :, :, 0].reshape(micro, TOK).astype(F32)
    routes = jnp.pad(routes, ((0, 8 - micro), (0, 128 - TOK)), constant_values=-1.0)
    pairs, count = 2 * micro, labels.shape[2]
    numbers = jnp.concatenate(
        [labels.reshape(pairs, count), frame_lengths.reshape(pairs, 1), label_lengths.reshape(pairs, 1)], axis=1
    )
    numbers = jnp.pad(numbers.astype(F32), ((0, 0), (0, 128 - numbers.shape[1])))
    losses, grad = run(
        frames.reshape(micro, TOK, D), w_in[0, 0], w_out[0, 0], router[0].T, norm_gain, routes,
        head_gain.reshape(1, D), head_weight.T, numbers,
    )
    return losses[0:1, 0:1], grad.T


def solution(mesh):
    placed = (
        P(None, ("expert", "dp"), None, None),
        P("section", None),
        P("section", None, None),
        P("section", "expert", None, None),
        P("section", "expert", None, None),
        P("section", None, ("expert", "dp"), None, None),
        P(),
        P(None, "expert"),
        P(None, ("expert", "dp")),
        P(None, ("expert", "dp"), None),
        P(None, ("expert", "dp")),
    )
    return jax.shard_map(
        per_device,
        mesh=mesh,
        in_specs=placed,
        out_specs=(P("section", ("expert", "dp")), P(None, "expert")),
        check_vma=False,
    )
```

```python
import functools

import jax
import jax.numpy as jnp
from jax import lax
from jax.experimental import pallas as pl
from jax.experimental.pallas import tpu as pltpu
from jax.sharding import PartitionSpec as P

EPSILON = 1e-06
LOG_ZERO = -1e30
MESH = pl.DeviceIdType.MESH
F32, BF16 = jnp.float32, jnp.bfloat16
D, HALF, EFF, LAYERS, RING, TOK, FRAMES = 1280, 640, 256, 8, 16, 96, 48
PIECES = 16
SKEW = 4
TURNS = PIECES // 4
CHUNKS = LAYERS * PIECES
IN_ROWS, OUT_ROWS = D // PIECES, EFF // PIECES
SHARD, WIDE = 500, 512
PART = WIDE // 2 // RING
HIGHEST = lax.Precision.HIGHEST
VMEM = pltpu.VMEM
DMA = pltpu.SemaphoreType.DMA
VMEM_LIMIT = 56 * 1024 * 1024
PLANE = sorted([(a, b) for a in range(4) for b in range(4) if a or b], key=lambda d: -sum(min(v, 4 - v) for v in d))
AROUND = sorted(range(1, RING), key=lambda d: -min(d, RING - d))


def coords():
    s, z, y = lax.axis_index("section"), lax.axis_index("expert"), lax.axis_index("dp")
    return s, s // 2, lax.rem(s, 2), z, y


def loop(low, high, body):
    def step(i, carry):
        body(i)
        return carry

    lax.fori_loop(low, high, step, 0)


def remote(src, dst, send, recv, device):
    return pltpu.make_async_remote_copy(
        src_ref=src, dst_ref=dst, send_sem=send, recv_sem=recv, device_id=device, device_id_type=MESH
    )


def dot(a, b, dims=((1,), (0,)), precision=None):
    return lax.dot_general(a, b, (dims, ((), ())), precision=precision, preferred_element_type=F32)


def rms(x, gain):
    return (x * lax.rsqrt(jnp.mean(x * x, axis=-1, keepdims=True) + EPSILON) * gain).astype(BF16)


def moe_kernel(
    frames, w_in, w_out, router, gain, routes, head_gain, hn_out,
    win, wout, aux, routers, auxes, state, give, take, answer, back, stage_in, stage_out, passed, landed,
    got_in, got_out, on_in, on_out, copy_in, copy_out, have_in, have_out,
    lay_send, stage_send, stage_got, small_send, small_got, give_send, take_got, answer_send, back_got, hn_send, hn_got, state_got,
):
    s, x, c, z, y = coords()
    me = 4 * x + y
    home_x, home_y = z // 4, lax.rem(z, 4)
    above, below = lax.rem(z + 1, RING), lax.rem(z + RING - 1, RING)
    barrier = pltpu.get_barrier_semaphore()

    def greet(i):
        p = lax.rem(4 * s + y + i, 32)
        pl.semaphore_signal(barrier, inc=1, device_id=(p // 4, z, lax.rem(p, 4)), device_id_type=MESH)

    for i in range(1, 32):
        greet(i)

    def greet_ring(i):
        pl.semaphore_signal(barrier, inc=1, device_id=(s, lax.rem(z + i, RING), y), device_id_type=MESH)

    for i in range(1, RING):
        greet_ring(i)
    pl.semaphore_wait(barrier, 46)

    def in_rows(j):
        return pl.ds(pl.multiple_of(j * IN_ROWS, 16), IN_ROWS)

    def out_rows(j):
        return pl.ds(pl.multiple_of(j * OUT_ROWS, 16), OUT_ROWS)

    def share(layer, i, src_in, src_out):
        j = y + 4 * i
        k = layer * PIECES + j
        target = (2 * home_x + 1, z, home_y)
        return (
            remote(src_in, win.at[layer, in_rows(j)], lay_send.at[2 * c, i], got_in.at[k], target),
            remote(src_out, wout.at[layer, out_rows(j)], lay_send.at[2 * c + 1, i], got_out.at[k], target),
        )

    def staged(i):
        j = y + 4 * i
        target = (s + 1, z, y)
        return (
            remote(w_in.at[in_rows(j)], stage_in.at[i], stage_send.at[0, i], stage_got.at[0, i], target),
            remote(w_out.at[out_rows(j)], stage_out.at[i], stage_send.at[1, i], stage_got.at[1, i], target),
        )

    def small(to_x):
        target = (2 * to_x, z, y)
        return (
            remote(aux, auxes.at[s], small_send.at[0, to_x], small_got.at[0, s], target),
            remote(router, routers.at[s], small_send.at[1, to_x], small_got.at[1, s], target),
        )

    def each(copies, act):
        for copy in copies:
            act(copy)

    start, sent, got = (lambda d: d.start()), (lambda d: d.wait_send()), (lambda d: d.wait_recv())

    @pl.when((c == 0) & (x == 0))
    def _():
        for i in range(TURNS):
            each(share(0, i, w_in.at[in_rows(y + 4 * i)], w_out.at[out_rows(y + 4 * i)]), start)

    @pl.when((c == 0) & (x > 0))
    def _():
        for i in range(TURNS):
            each(staged(i), start)

    rows, cols = lax.broadcasted_iota(jnp.int32, (128, 128), 0), lax.broadcasted_iota(jnp.int32, (128, 128), 1)
    aux[...] = jnp.zeros_like(aux)
    aux[0:1, :] = gain[...]
    for m in range(4):
        named = jnp.broadcast_to(routes[m : m + 1, :], (128, 128))
        before = (jnp.transpose(named) == named) & (rows < cols)
        rank = jnp.sum(before.astype(F32), axis=0, keepdims=True)
        live = lax.broadcasted_iota(jnp.int32, (1, 128), 1) < TOK
        aux[m + 1 : m + 2, 0:128] = jnp.where(live, 8.0 * routes[m : m + 1, :] + rank, -1.0)

    for gap in range(1, 4):
        each(small(lax.rem(x + gap, 4)), start)

    own_small = (
        pltpu.make_async_copy(aux, auxes.at[s], small_got.at[0, s]),
        pltpu.make_async_copy(router, routers.at[s], small_got.at[1, s]),
    )

    @pl.when(c == 1)
    def _():
        each(small(x), start)

    @pl.when(c == 0)
    def _():
        each(own_small, start)

    @pl.when(c == 1)
    def _():
        at_home = (x == home_x) & (y == home_y)
        up, down = lax.rem(z + RING - me, RING), lax.rem(me + RING - z, RING)

        def distribute(layer, slot, pick):
            for i in range(TURNS):
                j = y + 4 * i
                src_in, src_out = pick(i)

                @pl.when(at_home)
                def _():
                    k = layer * PIECES + j
                    pltpu.make_async_copy(src_in, win.at[layer, in_rows(j)], got_in.at[k]).start()
                    pltpu.make_async_copy(src_out, wout.at[layer, out_rows(j)], got_out.at[k]).start()

                @pl.when(jnp.logical_not(at_home))
                def _():
                    each(carried(layer, slot, i, src_in, src_out), start)

        def carried(layer, slot, i, src_in, src_out):
            j = y + 4 * i
            k = layer * PIECES + j
            target = (2 * home_x + 1, z, home_y)
            return (
                remote(src_in, win.at[layer, in_rows(j)], lay_send.at[2 * slot, i], got_in.at[k], target),
                remote(src_out, wout.at[layer, out_rows(j)], lay_send.at[2 * slot + 1, i], got_out.at[k], target),
            )

        def from_stage(i):
            return stage_in.at[i], stage_out.at[i]

        def from_own(i):
            return w_in.at[in_rows(y + 4 * i)], w_out.at[out_rows(y + 4 * i)]

        def rise(k):
            layer, j = k // PIECES, lax.rem(k, PIECES)
            ref = win.at[layer, in_rows(j)]
            return remote(ref, ref, on_in, got_in.at[k], (s, above, y))

        def sink(k):
            layer, j = k // PIECES, lax.rem(k, PIECES)
            ref = wout.at[layer, out_rows(j)]
            return remote(ref, ref, on_out, got_out.at[k], (s, below, y))

        def hand_in(layer):
            return remote(win.at[layer], win.at[layer], copy_in.at[layer], have_in.at[layer], (s - 1, z, y))

        def hand_out(layer):
            return remote(wout.at[layer], wout.at[layer], copy_out.at[layer], have_out.at[layer], (s - 1, z, y))

        def tick(t):
            @pl.when((x > 0) & (t == PIECES * (2 * x - 1)))
            def _():
                for i in range(TURNS):
                    each(staged(i), got)
                distribute(2 * x, 0, from_stage)

            @pl.when(t == 2 * PIECES * x)
            def _():
                distribute(2 * x + 1, 1, from_own)

            ku, kd = t - SKEW * up, t - SKEW * down

            @pl.when((ku >= 0) & (ku < CHUNKS))
            def _():
                rise(ku).wait_recv()

                @pl.when(up < RING - 1)
                def _():
                    rise(ku).start()

                @pl.when(lax.rem(ku, PIECES) == PIECES - 1)
                def _():
                    hand_in(ku // PIECES).start()

            @pl.when((kd >= 0) & (kd < CHUNKS))
            def _():
                sink(kd).wait_recv()

                @pl.when(down < RING - 1)
                def _():
                    sink(kd).start()

                @pl.when(lax.rem(kd, PIECES) == PIECES - 1)
                def _():
                    hand_out(kd // PIECES).start()

        loop(0, CHUNKS + SKEW * (RING - 1), tick)

        @pl.when(jnp.logical_not(at_home))
        def _():
            for i in range(TURNS):
                @pl.when(x > 0)
                def _():
                    each(carried(2 * x, 0, i, *from_stage(i)), sent)

                each(carried(2 * x + 1, 1, i, *from_own(i)), sent)

        @pl.when(up < RING - 1)
        def _():
            pltpu.make_async_copy(win, win, on_in).wait()

        @pl.when(down < RING - 1)
        def _():
            pltpu.make_async_copy(wout, wout, on_out).wait()

        loop(0, LAYERS, lambda layer: hand_in(layer).wait_send())
        loop(0, LAYERS, lambda layer: hand_out(layer).wait_send())
        each(small(x), sent)

    @pl.when(c == 0)
    def _():
        pltpu.make_async_copy(frames.at[x], state, state_got).start()

        def smalls(layer):
            pltpu.make_async_copy(aux, auxes.at[layer], small_got.at[0, layer]).wait()
            pltpu.make_async_copy(router, routers.at[layer], small_got.at[1, layer]).wait()

        loop(0, LAYERS, smalls)
        pltpu.make_async_copy(frames.at[x], state, state_got).wait()

        def chip(p):
            return (2 * (p // 4), z, lax.rem(p, 4))

        def out_to(p):
            return remote(give.at[p], take.at[me], give_send, take_got, chip(p))

        def back_to(p):
            return remote(answer.at[p], back.at[me], answer_send, back_got, chip(p))

        def start_all(copy):
            for i in range(1, RING):
                copy(lax.rem(me + i, RING)).start()

        def wait_all(buffer, sem):
            most = buffer.at[pl.ds(0, RING - 1)]
            pltpu.make_async_copy(most, most, sem).wait()

        def layer_step(layer):
            xf = state[...].astype(F32)
            normed = rms(xf, auxes[layer, 0:1, :])
            which = lax.broadcasted_iota(jnp.int32, (8, 128), 0) == 1 + x
            spots = jnp.sum(jnp.where(which, auxes[layer, :, 0:128], 0.0), axis=0, keepdims=True)
            pick = (lax.broadcasted_iota(jnp.int32, (128, 128), 0).astype(F32) == spots)[:, :TOK]
            pick = pick.astype(F32).astype(BF16)
            left = dot(pick, normed[:, :HALF]).reshape(RING, 8, HALF)
            right = dot(pick, normed[:, HALF:]).reshape(RING, 8, HALF)
            give[...] = jnp.concatenate([left, right], axis=1).astype(BF16)
            start_all(out_to)
            take[me] = give[me]

            columns = jnp.transpose(jnp.broadcast_to(spots, (128, 128)))[:TOK, :].astype(jnp.int32)
            lane = lax.broadcasted_iota(jnp.int32, (TOK, 128), 1)
            logits = dot(normed, routers[layer], ((1,), (1,)))
            mine = (lane[:, :RING] == (columns[:, :RING] >> 3)).astype(F32)
            gate = jax.nn.sigmoid(jnp.sum(mine * logits, axis=1, keepdims=True))
            place = columns + ((columns >> 3) << 3)
            spread = [(lane + 128 * h == place + 8 * b).astype(F32).astype(BF16) for b in range(2) for h in range(2)]
            put_left = jnp.concatenate(spread[:2], axis=1)
            put_right = jnp.concatenate(spread[2:], axis=1)

            pltpu.make_async_copy(win.at[layer], win.at[layer], have_in.at[layer]).wait()
            wait_all(take, take_got)
            rows = take[...].reshape(RING * 16, HALF)
            first = dot(rows, win[layer, 0:HALF, :]).reshape(RING, 16, EFF)
            second = dot(rows, win[layer, HALF:D, :]).reshape(RING, 16, EFF)
            hidden = (first[:, 0:8] + second[:, 8:16]).reshape(128, EFF)
            active = (hidden * jax.nn.sigmoid(hidden)).astype(BF16)
            pltpu.make_async_copy(wout.at[layer], wout.at[layer], have_out.at[layer]).wait()
            result = dot(active, wout[layer]).reshape(RING, 8, D)
            answer[...] = jnp.concatenate([result[:, :, :HALF], result[:, :, HALF:]], axis=1).astype(BF16)
            start_all(back_to)
            back[me] = answer[me]
            wait_all(give, give_send)
            wait_all(back, back_got)
            returned = back[...].reshape(RING * 16, HALF)
            mixed = jnp.concatenate([dot(put_left, returned), dot(put_right, returned)], axis=1)
            state[...] = (xf + gate * mixed).astype(BF16)
            wait_all(answer, answer_send)

        loop(0, LAYERS, layer_step)
        hn = rms(state[...].astype(F32), head_gain[...].reshape(1, D))
        for h in range(2):
            hn_out[h] = hn[:FRAMES, HALF * h : HALF * (h + 1)]
            passed[h] = hn[FRAMES:, HALF * h : HALF * (h + 1)]
        remote(passed, landed, hn_send, hn_got, (s + 1, z, y)).start()

        @pl.when(x == 0)
        def _():
            for i in range(TURNS):
                each(share(0, i, w_in.at[in_rows(y + 4 * i)], w_out.at[out_rows(y + 4 * i)]), sent)

        @pl.when(x > 0)
        def _():
            for i in range(TURNS):
                each(staged(i), sent)

        remote(passed, landed, hn_send, hn_got, (s + 1, z, y)).wait_send()

    @pl.when(c == 1)
    def _():
        remote(passed, landed, hn_send, hn_got, (s, z, y)).wait_recv()
        hn_out[...] = landed[...]

    for gap in range(1, 4):
        each(small(lax.rem(x + gap, 4)), sent)


def flip(block):
    rows = block.shape[0]
    if rows < 128:
        block = jnp.concatenate([block, jnp.zeros((128 - rows, 128), F32)], axis=0)
    return jnp.transpose(block)


def pack(columns):
    turned = flip(columns)
    return turned[0:8] + pltpu.roll(turned[8:16], 64, 1)


def lanes(rows):
    return lax.broadcasted_iota(jnp.int32, (rows, 128), 1)


def triple(a, b, c):
    top = jnp.maximum(jnp.maximum(a, b), c)
    return top + jnp.log(jnp.exp(a - top) + jnp.exp(b - top) + jnp.exp(c - top))


def head_kernel(
    fetch, hn, weight, numbers, loss_out, grad_out,
    rows_all, names, names_all, chosen_all, logits, stats, stats_all, emit, ahead, behind, notes, notes_all, grads, partial,
    half_out, half_in, pieces, pieces_all, total, totals,
    up_send, up_got, down_send, down_got, name_send, name_got, stat_send, stat_got, note_send, note_got,
    half_send, half_got, piece_send, piece_got, total_send, total_got, last_send, last_got,
):
    s, x, c, z, y = coords()
    me = 4 * x + y
    pair = (s + 1 - 2 * c, z, y)
    above, below = lax.rem(z + 1, RING), lax.rem(z + RING - 1, RING)

    def chip(p):
        return (2 * (p // 4) + c, z, lax.rem(p, 4))

    def along(act):
        for i in AROUND:
            act(lax.rem(z + i, RING))

    def across(act):
        for a, b in PLANE:
            act(4 * lax.rem(x + a, 4) + lax.rem(y + b, 4))

    def rise(i, h):
        block = rows_all.at[lax.rem(z + RING - i, RING), h]
        return remote(block, block, up_send.at[i, h], up_got.at[i, h], (s, above, y))

    def sink(i, h):
        block = rows_all.at[lax.rem(z + i, RING), h]
        return remote(block, block, down_send.at[i, h], down_got.at[i, h], (s, below, y))

    def risen(i, h):
        block = rows_all.at[lax.rem(z + RING - i, RING), h]
        return remote(block, block, up_send.at[i - 1, h], up_got.at[i - 1, h], (s, above, y))

    def sunk(i, h):
        block = rows_all.at[lax.rem(z + i, RING), h]
        return remote(block, block, down_send.at[i - 1, h], down_got.at[i - 1, h], (s, below, y))

    rows_all[z] = hn[...]
    for h in range(2):
        rise(0, h).start()
        sink(0, h).start()

    one = lanes(1)
    chosen = lax.broadcasted_iota(jnp.int32, (8, 128), 0) == s
    known_row = jnp.sum(jnp.where(chosen, numbers[...], 0.0), axis=0, keepdims=True)
    tags = jnp.where(one < 12, known_row, jnp.where(one == 12, 0.0, -2.0))
    names[...] = jnp.broadcast_to(tags, (8, 128))

    def all_but_one(buffer, sem):
        most = buffer.at[pl.ds(0, RING - 1)]
        pltpu.make_async_copy(most, most, sem).wait()

    def name_to(p):
        return remote(names, names_all.at[z], name_send, name_got, (s, p, y))

    along(lambda p: name_to(p).start())
    fetch.wait()
    names_all[z] = names[...]
    logits[:, WIDE - 128 : WIDE] = jnp.zeros((RING * FRAMES, 128), F32)

    columns = lax.broadcasted_iota(jnp.int32, (128, WIDE), 1)
    valid = columns[:FRAMES] < SHARD
    owned = jnp.where(columns < SHARD, columns + SHARD * z, -1).astype(F32)

    def selector(k):
        wanted = flip(jnp.broadcast_to(names_all[k, 0:1, :], (128, 128)))
        return (jnp.concatenate([wanted] * 4, axis=1) == owned).astype(F32).astype(BF16)

    def thirds(value):
        high = value.astype(BF16)
        rest = value - high.astype(F32)
        middle = rest.astype(BF16)
        return jnp.concatenate([high, middle, (rest - middle.astype(F32)).astype(BF16)], axis=0)

    def joined(parts):
        return parts[0:FRAMES] + parts[FRAMES : 2 * FRAMES] + parts[2 * FRAMES :]

    def frames_of(k):
        return pl.ds(pl.multiple_of(k * FRAMES, FRAMES), FRAMES)

    lane = lanes(FRAMES)

    def stat_to(p):
        return remote(stats.at[p], stats_all.at[z], stat_send, stat_got, (s, p, y))

    def evaluate(blocks):
        def side(h):
            return jnp.concatenate([rows_all[k, h] for k in blocks], axis=0)

        value = dot(side(0), weight[:, 0:HALF], ((1,), (1,))) + dot(side(1), weight[:, HALF:D], ((1,), (1,)))
        for n, k in enumerate(blocks):
            logits[frames_of(k), 0:SHARD] = value[n * FRAMES : (n + 1) * FRAMES]
        for k in blocks:
            block = logits[frames_of(k), :]
            peak = jnp.max(jnp.where(valid, block, -jnp.inf), axis=1, keepdims=True)
            weightsum = jnp.sum(jnp.where(valid, jnp.exp(block - peak), 0.0), axis=1, keepdims=True)
            chosen_all[k] = selector(k)
            found = joined(dot(thirds(block), chosen_all[k], ((1,), (1,))))
            stats[k] = pack(jnp.where(lane == 13, peak, jnp.where(lane == 14, weightsum, found)))

    def ring_step(i):
        for h in range(2):
            risen(i, h).wait_recv()

            @pl.when(i < 8)
            def _():
                rise(i, h).start()
                sunk(i, h).wait_recv()

            @pl.when(i < 7)
            def _():
                sink(i, h).start()

        @pl.when(i == 1)
        def _():
            all_but_one(names_all, name_got)

        lower, upper = lax.rem(z + RING + 1 - i, RING), lax.rem(z + i - 1, RING)
        evaluate((lower, upper))

        @pl.when(i > 1)
        def _():
            stat_to(lower).start()
            stat_to(upper).start()

    loop(1, 9, ring_step)
    opposite = lax.rem(z + 8, RING)
    evaluate((opposite,))
    stat_to(opposite).start()
    stats_all[z] = stats[z]
    all_but_one(stats_all, stat_got)

    low = [stats_all[k] for k in range(RING)]
    high = [pltpu.roll(v, 64, 1) for v in low]
    peaks = functools.reduce(jnp.maximum, high)
    sums = sum(v * pltpu.roll(jnp.exp(v - peaks), 1, 0) for v in high)
    live = lanes(1) < FRAMES
    log_total = jnp.where(live, peaks[5:6] + jnp.log(jnp.where(live, sums[6:7], 1.0)), 0.0)
    both = jnp.concatenate([sum(low), sum(high)], axis=0)
    slot = lax.broadcasted_iota(jnp.int32, (16, 128), 0)
    both = jnp.where(lanes(16) < FRAMES, both - log_total, 0.0)
    both = jnp.where(slot < 13, both, jnp.where(slot == 14, log_total, 0.0))
    by_label = flip(both)
    row, col = lax.broadcasted_iota(jnp.int32, (128, 128), 0), lanes(128)
    odd = (col & 1) == 1
    expand = (col < 25) & (jnp.where(odd, col >> 1, 12) == row)
    expand = expand.astype(F32)
    emit[...] = dot(by_label[:FRAMES], expand, precision=HIGHEST)
    total_col = by_label[:FRAMES]
    span = jnp.sum(jnp.where(one == 12, known_row, 0.0), axis=1, keepdims=True)
    last = 2.0 * jnp.sum(jnp.where(one == 13, known_row, 0.0), axis=1, keepdims=True)
    differs = (known_row != pltpu.roll(known_row, 1, 1)) & (known_row != 0.0) & (one > 0) & (one < 12)
    jumps = dot(jnp.broadcast_to(differs.astype(F32), (8, 128)), expand)[0:1]
    jump, jump_back = jumps > 0.5, pltpu.roll(jumps, 126, 1) > 0.5
    spot = one.astype(F32)
    ends = (spot == last) | (spot == last - 1.0)
    closing = jnp.where(ends, 0.0, LOG_ZERO)
    opening = jnp.where(one < 2, emit[0:1, :], LOG_ZERO)
    ahead[0:1, :] = opening
    behind[FRAMES - 1 : FRAMES, :] = closing

    def ctc_step(i, carry):
        a, b = carry
        once = jnp.where(one < 1, LOG_ZERO, pltpu.roll(a, 1, 1))
        twice = jnp.where(jump, pltpu.roll(a, 2, 1), LOG_ZERO)
        moved = triple(a, once, twice) + emit[pl.ds(i, 1), :]
        a = jnp.where(i.astype(F32) < span, moved, a)
        ahead[pl.ds(i, 1), :] = a
        t = FRAMES - 1 - i
        g = b + emit[pl.ds(t + 1, 1), :]
        once = jnp.where(one > 126, LOG_ZERO, pltpu.roll(g, 127, 1))
        twice = jnp.where(jump_back, pltpu.roll(g, 126, 1), LOG_ZERO)
        b = jnp.where(t.astype(F32) < span - 1.0, triple(g, once, twice), closing)
        behind[pl.ds(t, 1), :] = b
        return a, b

    final, _ = lax.fori_loop(1, FRAMES, ctc_step, (opening, closing))
    tail = jnp.where(ends, final, LOG_ZERO)
    top = jnp.max(tail, axis=1, keepdims=True)
    likely = top + jnp.log(jnp.sum(jnp.where(ends, jnp.exp(final - top), 0.0), axis=1, keepdims=True))
    loss_out[...] = -likely
    when = lax.broadcasted_iota(jnp.int32, (FRAMES, 128), 0).astype(F32)
    occupied = jnp.where(
        (when < span) & (lane < 25), -jnp.exp(ahead[...] + behind[...] - likely), 0.0
    )
    merged = dot(occupied, expand, ((1,), (1,)), HIGHEST)
    mass = jnp.sum(occupied, axis=1, keepdims=True)
    notes[...] = pack(
        jnp.where(lane == 13, mass, jnp.where(lane == 14, total_col, jnp.where(lane < 13, merged, 0.0)))
    )
    notes_all[z] = notes[...]

    def note_to(p):
        return remote(notes, notes_all.at[z], note_send, note_got, (s, p, y))

    along(lambda p: note_to(p).start())
    all_but_one(notes_all, note_got)

    def spread(group):
        for k in [4 * group + n for n in range(4)]:
            packed = notes_all[k]
            known = flip(jnp.concatenate([packed, pltpu.roll(packed, 64, 1)], axis=0))[:FRAMES]
            scattered = joined(dot(thirds(known), chosen_all[k]))
            block = logits[frames_of(k), :]
            value = scattered - jnp.exp(block - known[:, 14:15]) * known[:, 13:14]
            grads[frames_of(k), :] = jnp.where(valid, value, 0.0).astype(BF16)

    loop(0, RING // 4, spread)
    for h in range(2):
        partial[:, HALF * h : HALF * (h + 1)] = dot(
            grads[...], rows_all[:, h].reshape(RING * FRAMES, HALF), ((0,), (0,))
        )

    def mine(core):
        return pl.ds(pl.multiple_of(256 * core, 256), 256)

    half_out[...] = partial[mine(1 - c), :].astype(BF16)
    swap = remote(half_out, half_in, half_send, half_got, pair)
    swap.start()
    swap.wait_recv()
    pieces[...] = (partial[mine(c), :] + half_in[...].astype(F32)).astype(BF16).reshape(RING, PART, D)

    def piece_to(p):
        return remote(pieces.at[p], pieces_all.at[me], piece_send, piece_got, chip(p))

    across(lambda p: piece_to(p).start())
    pieces_all[me] = pieces[me]
    all_but_one(pieces_all, piece_got)
    total[...] = sum(pieces_all[k].astype(F32) for k in range(RING)).astype(BF16)

    def pass_on(p):
        return remote(totals.at[c, p], totals.at[c, p], last_send, last_got, pair)

    for n, (a, b) in enumerate(PLANE):
        p = 4 * lax.rem(x + a, 4) + lax.rem(y + b, 4)
        remote(total, totals.at[c, me], total_send, total_got.at[n // 5], chip(p)).start()
    totals[c, me] = total[...]
    pass_on(me).start()
    for g in range(3):
        five = pieces.at[pl.ds(0, 5)]
        pltpu.make_async_copy(five, five, total_got.at[g]).wait()
        for a, b in PLANE[5 * g : 5 * g + 5]:
            pass_on(4 * lax.rem(x + 4 - a, 4) + lax.rem(y + 4 - b, 4)).start()
    pltpu.make_async_copy(totals.at[1 - c], totals.at[1 - c], last_got).wait()
    grad_out[0:256, :] = totals[0].reshape(256, D)
    grad_out[256:SHARD, :] = totals[1].reshape(256, D)[: SHARD - 256, :]

    pltpu.make_async_copy(totals.at[c], totals.at[c], last_send).wait()
    swap.wait_send()
    all_but_one(names_all, name_send)
    all_but_one(stats, stat_send)
    all_but_one(notes_all, note_send)
    all_but_one(pieces, piece_send)
    all_but_one(pieces, total_send)

    def ring_sent(i):
        for h in range(2):
            rise(i, h).wait_send()

            @pl.when(i < 7)
            def _():
                sink(i, h).wait_send()

    loop(0, 8, ring_sent)


MOE_SCRATCH = [
    VMEM((LAYERS, D, EFF), BF16),
    VMEM((LAYERS, EFF, D), BF16),
    VMEM((8, D), F32),
    VMEM((LAYERS, 16, D), BF16),
    VMEM((LAYERS, 8, D), F32),
    VMEM((TOK, D), BF16),
    VMEM((RING, 16, HALF), BF16),
    VMEM((RING, 16, HALF), BF16),
    VMEM((RING, 16, HALF), BF16),
    VMEM((RING, 16, HALF), BF16),
    VMEM((TURNS, IN_ROWS, EFF), BF16),
    VMEM((TURNS, OUT_ROWS, D), BF16),
    VMEM((2, FRAMES, HALF), BF16),
    VMEM((2, FRAMES, HALF), BF16),
    DMA((CHUNKS,)), DMA((CHUNKS,)), DMA, DMA,
    DMA((LAYERS,)), DMA((LAYERS,)), DMA((LAYERS,)), DMA((LAYERS,)),
    DMA((4, TURNS)), DMA((2, TURNS)), DMA((2, TURNS)), DMA((2, 4)), DMA((2, LAYERS)),
    DMA, DMA, DMA, DMA,
    DMA, DMA, DMA,
]
HEAD_SCRATCH = [
    VMEM((RING, 2, FRAMES, HALF), BF16),
    VMEM((8, 128), F32),
    VMEM((RING, 8, 128), F32),
    VMEM((RING, 128, WIDE), BF16),
    VMEM((RING * FRAMES, WIDE), F32),
    VMEM((RING, 8, 128), F32),
    VMEM((RING, 8, 128), F32),
    VMEM((FRAMES, 128), F32),
    VMEM((FRAMES, 128), F32),
    VMEM((FRAMES, 128), F32),
    VMEM((8, 128), F32),
    VMEM((RING, 8, 128), F32),
    VMEM((RING * FRAMES, WIDE), BF16),
    VMEM((WIDE, D), F32),
    VMEM((256, D), BF16),
    VMEM((256, D), BF16),
    VMEM((RING, PART, D), BF16),
    VMEM((RING, PART, D), BF16),
    VMEM((PART, D), BF16),
    VMEM((2, RING, PART, D), BF16),
    DMA((8, 2)), DMA((8, 2)), DMA((8, 2)), DMA((8, 2)),
    DMA, DMA, DMA, DMA, DMA, DMA,
    DMA, DMA,
    DMA, DMA, DMA, DMA((3,)),
    DMA, DMA,
]


def whole_kernel(
    frames, w_in, w_out, router, gain, routes, head_gain, head_weight, numbers, loss_out, grad_out,
    hn, weight, weight_got, *scratch,
):
    fetch = pltpu.make_async_copy(head_weight, weight, weight_got)
    fetch.start()
    moe_kernel(frames, w_in, w_out, router, gain, routes, head_gain, hn, *scratch[: len(MOE_SCRATCH)])
    head_kernel(fetch, hn, weight, numbers, loss_out, grad_out, *scratch[len(MOE_SCRATCH) :])


def run(*arrays):
    anywhere, local = pl.BlockSpec(memory_space=pl.ANY), pl.BlockSpec(memory_space=VMEM)
    return pl.pallas_call(
        whole_kernel,
        out_shape=(jax.ShapeDtypeStruct((1, 1), F32), jax.ShapeDtypeStruct((SHARD, D), BF16)),
        in_specs=[anywhere] * 3 + [local] * 4 + [anywhere, local],
        out_specs=(local, local),
        scratch_shapes=[VMEM((2, FRAMES, HALF), BF16), VMEM((SHARD, D), BF16), DMA] + MOE_SCRATCH + HEAD_SCRATCH,
        compiler_params=pltpu.CompilerParams(
            collective_id=0, has_side_effects=True, vmem_limit_bytes=VMEM_LIMIT
        ),
    )(*arrays)


def per_device(
    frames,
    norm_gain,
    router,
    w_in,
    w_out,
    routing,
    head_gain,
    head_weight,
    frame_lengths,
    labels,
    label_lengths,
):
    micro = frames.shape[0]
    routes = routing[0, :, :, :, 0].reshape(micro, TOK).astype(F32)
    routes = jnp.pad(routes, ((0, 8 - micro), (0, 128 - TOK)), constant_values=-1.0)
    pairs, count = 2 * micro, labels.shape[2]
    numbers = jnp.concatenate(
        [labels.reshape(pairs, count), frame_lengths.reshape(pairs, 1), label_lengths.reshape(pairs, 1)], axis=1
    )
    numbers = jnp.pad(numbers.astype(F32), ((0, 0), (0, 128 - numbers.shape[1])))
    losses, grad = run(
        frames.reshape(micro, TOK, D), w_in[0, 0], w_out[0, 0], router[0].T, norm_gain, routes,
        head_gain, head_weight.T, numbers,
    )
    return losses, grad.T


def solution(mesh):
    placed = (
        P(None, ("expert", "dp"), None, None),
        P("section", None),
        P("section", None, None),
        P("section", "expert", None, None),
        P("section", "expert", None, None),
        P("section", None, ("expert", "dp"), None, None),
        P(),
        P(None, "expert"),
        P(None, ("expert", "dp")),
        P(None, ("expert", "dp"), None),
        P(None, ("expert", "dp")),
    )
    return jax.shard_map(
        per_device,
        mesh=mesh,
        in_specs=placed,
        out_specs=(P("section", ("expert", "dp")), P(None, "expert")),
        check_vma=False,
    )
```
